32 devices in a mesh: kv: 2 (over x), seq: 16 (over z, y, core).
Axes of the slice: x: 2, y: 2, z: 4, core: 2. Of those that a mesh axis runs over, the one named last changes fastest.
Arguments:
- queries: bfloat16 [512, 1024], P(('kv', 'seq')), may hold values from -6 to 6
- out_grad: bfloat16 [512, 1024], P(('kv', 'seq')), may hold values from -768 to 768
- saved_out: bfloat16 [512, 1024], P(('kv', 'seq')), may hold values from -1.5 to 1.5
- saved_lse: float32 [512, 8], P(('kv', 'seq')), as said below
- video_keys: bfloat16 [4096, 256], P('seq', 'kv'), may hold values from -6 to 6
- video_values: bfloat16 [4096, 256], P('seq', 'kv'), may hold values from -6 to 6
Outputs:
- grad_queries: bfloat16 [512, 1024], P(('kv', 'seq'))
- grad_keys: bfloat16 [4096, 256], P('seq', 'kv')
- grad_values: bfloat16 [4096, 256], P('seq', 'kv')
The draws below stay inside these ranges and needn't reach their ends.
Inputs may be any that keep to these rules, and one draw needn't show every extreme that they name: saved_lse lies between log(4096) and log(4096) + 1.5.
All inputs are finite; a program needn't handle non-finite values.
Results may differ from the reference program's by a relative error of at most 0.0057.
Values may be sent and summed in bfloat16 or wider, within the bound.
No kernel may reach another device: no remote copies, remote signals or barrier semaphores. Data moves between devices by JAX's collectives and lax.ppermute only.
A program may use at most 64 MiB of HBM per device.

```python
import math
import jax
import jax.numpy as jnp

HD = 128
GROUP = 4
QUERIES = 512
KV_HEADS = 2
HEADS = 8
KEYS = 4096


def draw_saved_lse(key, part):
    log_keys = jnp.log(jnp.float32(KEYS))
    offsets = jax.random.uniform(key, (QUERIES, HEADS), jnp.float32, 0.3, 1.2)
    return log_keys + offsets


def steps_of(stream_key, shape, cuts, least, largest):
    loudness = 1.0
    for axis_at, shards_of in cuts:
        heights = jax.random.uniform(jax.random.fold_in(jax.random.fold_in(stream_key, 6), axis_at), (shards_of,), jnp.float32, least / len(cuts), largest / len(cuts))
        loudness = loudness * jnp.repeat(jnp.exp(heights), shape[axis_at] // shards_of).reshape((-1,) + (1,) * (len(shape) - 1 - axis_at))
    return loudness


def noise(rng, shape, width, limit, cuts=(), kind=jnp.bfloat16):
    result = width * jax.random.normal(rng, shape, jnp.float32)
    if cuts:
        result = result * steps_of(rng, shape, cuts, -0.22, 0.18)
    return jnp.clip(result, -limit, limit).astype(kind)


def setup_inputs(seed: int = 0) -> dict:
    key_list = jax.random.split(jax.random.key(seed), 7)
    return {
        "queries": noise(key_list[0], (QUERIES, HEADS * HD), 1.0, 6.0, ((0, 32),)),
        "out_grad": noise(key_list[1], (QUERIES, HEADS * HD), (KEYS // 32), 768.0, ((0, 32),)),
        "saved_out": noise(key_list[2], (QUERIES, HEADS * HD), 0.25, 1.5, ((0, 32),)),
        "saved_lse": draw_saved_lse(jax.random.fold_in(key_list[6], 71), 0),
        "video_keys": noise(key_list[4], (KEYS, KV_HEADS * HD), 1.0, 6.0, ((0, 16), (1, 2))),
        "video_values": noise(key_list[5], (KEYS, KV_HEADS * HD), 1.0, 6.0, ((0, 16), (1, 2))),
    }


def reference(queries, out_grad, saved_out, saved_lse, video_keys, video_values):
    score_scale = 1.0 / math.sqrt(HD)
    products = out_grad.astype(jnp.float32) * saved_out.astype(jnp.float32)
    row_delta = products.reshape(QUERIES, HEADS, HD).sum(axis=2)
    query_columns = []
    key_columns = []
    value_columns = []
    for kv_index in range(KV_HEADS):
        key_block = video_keys[:, kv_index * HD:(kv_index + 1) * HD]
        value_block = video_values[:, kv_index * HD:(kv_index + 1) * HD]
        key_total = jnp.zeros((KEYS, HD), jnp.float32)
        value_total = jnp.zeros((KEYS, HD), jnp.float32)
        for member in range(GROUP):
            head_index = kv_index * GROUP + member
            query_head = queries[:, head_index * HD:(head_index + 1) * HD]
            grad_head = out_grad[:, head_index * HD:(head_index + 1) * HD]
            scores = jnp.dot(query_head, key_block.T, preferred_element_type=jnp.float32) * score_scale
            probs = jnp.exp(scores - saved_lse[:, head_index:head_index + 1])
            probs_half = probs.astype(jnp.bfloat16)
            value_total = value_total + jnp.dot(probs_half.T, grad_head, preferred_element_type=jnp.float32)
            dprobs = jnp.dot(grad_head, value_block.T, preferred_element_type=jnp.float32)
            dscores = (probs * (dprobs - row_delta[:, head_index:head_index + 1])).astype(jnp.bfloat16)
            key_total = key_total + jnp.dot(dscores.T, query_head, preferred_element_type=jnp.float32)
            query_columns.append((jnp.dot(dscores, key_block, preferred_element_type=jnp.float32) * score_scale).astype(jnp.bfloat16))
        key_columns.append((key_total * score_scale).astype(jnp.bfloat16))
        value_columns.append(value_total.astype(jnp.bfloat16))
    return (jnp.concatenate(query_columns, axis=1), jnp.concatenate(key_columns, axis=1), jnp.concatenate(value_columns, axis=1))
```

```python
import functools
import math

import jax
import jax.numpy as jnp
from jax import lax
from jax.experimental import pallas as pl
from jax.experimental.pallas import tpu as pltpu
from jax.sharding import PartitionSpec as P

LANES = 128
PIECES = 3
VMEM_BYTES = 32 * 1024 * 1024


def vmem(count):
    return [pl.BlockSpec(memory_space=pltpu.VMEM)] * count


def bf16(value):
    return value.astype(jnp.bfloat16)


def f32(value):
    return value.astype(jnp.float32)


def pack_kernel(
    heads, groups, score_scale,
    queries, out_grad, saved_out, saved_lse, keys, values, rows_out, pairs_out,
):
    own_rows, width = queries.shape
    group_width = width // groups
    group_heads = heads // groups
    group = lax.axis_index("kv")
    pairs_out[:, : keys.shape[1]] = keys[...]
    pairs_out[:, keys.shape[1] :] = values[...]
    for step in range(groups):
        source = lax.rem(group + step, groups)
        columns = pl.ds(pl.multiple_of(source * group_width, group_width), group_width)
        rows_out[:, step * group_width : (step + 1) * group_width] = queries[:, columns]
        rows_out[:, width + step * group_width : width + (step + 1) * group_width] = out_grad[:, columns]
    lane = lax.broadcasted_iota(jnp.int32, (own_rows, LANES), 1)
    stats = jnp.zeros((own_rows, LANES), jnp.float32)
    products = f32(out_grad[...]) * f32(saved_out[...])
    head_width = width // heads
    for head in range(heads):
        place = lax.rem(head - group * group_heads + heads, heads) * PIECES
        delta = jnp.sum(products[:, head * head_width : (head + 1) * head_width], axis=1, keepdims=True)
        shift = saved_lse[:, head : head + 1] * (1.0 / score_scale)
        stats = jnp.where((lane >= place) & (lane < place + PIECES), shift, stats)
        place = place + heads * PIECES
        stats = jnp.where((lane >= place) & (lane < place + PIECES), delta, stats)
    piece = lax.rem(lane, PIECES)
    first = f32(bf16(stats))
    second = f32(bf16(stats - first))
    third = stats - first - second
    rows_out[:, 2 * width :] = bf16(jnp.where(piece == 0, first, jnp.where(piece == 1, second, third)))


def pack(queries, out_grad, saved_out, saved_lse, keys, values, groups, score_scale):
    own_rows, width = queries.shape
    heads = saved_lse.shape[1]
    return pl.pallas_call(
        functools.partial(pack_kernel, heads, groups, score_scale),
        out_shape=(
            jax.ShapeDtypeStruct((own_rows, 2 * width + LANES), jnp.bfloat16),
            jax.ShapeDtypeStruct((keys.shape[0], 2 * keys.shape[1]), jnp.bfloat16),
        ),
        in_specs=vmem(6),
        out_specs=tuple(vmem(2)),
        compiler_params=pltpu.CompilerParams(vmem_limit_bytes=VMEM_BYTES),
    )(queries, out_grad, saved_out, saved_lse, keys, values)


def dot(left, right, left_dim, right_dim):
    return lax.dot_general(
        left, right, (((left_dim,), (right_dim,)), ((), ())), preferred_element_type=jnp.float32
    )


def attend_kernel(heads, groups, score_scale, row_blocks, pair_blocks, *refs):
    rows = refs[:row_blocks]
    pairs = refs[row_blocks : row_blocks + pair_blocks]
    dq_own, dq_other, *dpairs = refs[row_blocks + pair_blocks :]
    block_rows = rows[0].shape[0]
    width = (rows[0].shape[1] - LANES) // 2
    head_width = width // heads
    group_heads = heads // groups
    half = row_blocks // 2 * block_rows
    key_rows = pairs[0].shape[0]
    per_group = pair_blocks // groups
    exponent = score_scale * math.log2(math.e)
    lane = lax.broadcasted_iota(jnp.int32, (row_blocks * block_rows, LANES), 1)
    stats = jnp.concatenate([block[:, 2 * width :] for block in rows], axis=0)
    none = jnp.zeros_like(stats)
    minus = jnp.full((per_group * key_rows, LANES), -1.0, jnp.bfloat16)
    for group in range(groups):
        members = pairs[group * per_group : (group + 1) * per_group]
        keys = jnp.concatenate([pair[:, :head_width] for pair in members], axis=0)
        values = jnp.concatenate([pair[:, head_width:] for pair in members], axis=0)
        keys_wide = jnp.concatenate([keys, minus], axis=1)
        values_wide = jnp.concatenate([values, minus], axis=1)
        dkeys = dvalues = None
        for member in range(group_heads):
            head = group * group_heads + member
            columns = slice(head * head_width, (head + 1) * head_width)
            query = jnp.concatenate([block[:, columns] for block in rows], axis=0)
            columns = slice(width + head * head_width, width + (head + 1) * head_width)
            grad = jnp.concatenate([block[:, columns] for block in rows], axis=0)
            first = head * PIECES
            shift = jnp.where((lane >= first) & (lane < first + PIECES), stats, none)
            first = (heads + head) * PIECES
            delta = jnp.where((lane >= first) & (lane < first + PIECES), stats, none)
            scores = dot(keys_wide, jnp.concatenate([query, shift], axis=1), 1, 1)
            probs = jnp.exp2(scores * exponent)
            dprobs = dot(values_wide, jnp.concatenate([grad, delta], axis=1), 1, 1)
            dscores = bf16(probs * dprobs)
            dvalue = dot(bf16(probs), grad, 1, 0)
            dkey = dot(dscores, query, 1, 0)
            dvalues = dvalue if dvalues is None else dvalues + dvalue
            dkeys = dkey if dkeys is None else dkeys + dkey
            dquery = dot(dscores, keys, 0, 0) * score_scale
            columns = slice(head * head_width, (head + 1) * head_width)
            dq_own[:, columns] = dquery[:half]
            dq_other[:, columns] = bf16(dquery[half:])
        dkeys = dkeys * score_scale
        for index in range(per_group):
            out = dpairs[group * per_group + index]
            place = slice(index * key_rows, (index + 1) * key_rows)
            out[:, :head_width] = dkeys[place].astype(out.dtype)
            out[:, head_width:] = dvalues[place].astype(out.dtype)


def attend(rows, pairs, heads, groups, score_scale):
    block_rows, packed = rows[0].shape
    width = (packed - LANES) // 2
    half = len(rows) // 2 * block_rows
    outs = [
        jax.ShapeDtypeStruct((half, width), jnp.float32),
        jax.ShapeDtypeStruct((half, width), jnp.bfloat16),
        jax.ShapeDtypeStruct(pairs[0].shape, jnp.float32),
    ] + [jax.ShapeDtypeStruct(pairs[0].shape, jnp.bfloat16)] * (len(pairs) - 1)
    return pl.pallas_call(
        functools.partial(attend_kernel, heads, groups, score_scale, len(rows), len(pairs)),
        out_shape=tuple(outs),
        in_specs=vmem(len(rows) + len(pairs)),
        out_specs=tuple(vmem(len(outs))),
        compiler_params=pltpu.CompilerParams(vmem_limit_bytes=VMEM_BYTES),
    )(*rows, *pairs)


def turn_seq(array, seq_count, target):
    return lax.ppermute(array, "seq", [(place, target(place)) for place in range(seq_count)])


def planes(queries, out_grad, saved_out, saved_lse, video_keys, video_values):
    groups = lax.axis_size("kv")
    seq_count = lax.axis_size("seq")
    outer = seq_count // 4
    own_rows, width = queries.shape
    heads = saved_lse.shape[1]
    head_width = video_keys.shape[1]
    score_scale = 1.0 / math.sqrt(head_width)

    def along(array, step):
        return turn_seq(array, seq_count, lambda place: (place // 4 + step) % outer * 4 + place % 4)

    def other_core(array):
        return turn_seq(array, seq_count, lambda place: place ^ 1)

    def middle(array):
        return turn_seq(array, seq_count, lambda place: place ^ 2)

    def across(array):
        return lax.ppermute(array, "kv", [(0, 1), (1, 0)])

    def diagonal(array):
        steps = [
            (kv * seq_count + place, (1 - kv) * seq_count + (place ^ 2))
            for kv in range(2)
            for place in range(seq_count)
        ]
        return lax.ppermute(array, ("kv", "seq"), steps)

    sends = (middle, across, diagonal)
    packed, pair = pack(
        queries, out_grad, saved_out, saved_lse, video_keys, video_values, groups, score_scale
    )
    pairs = [pair] + [send(pair) for send in sends]
    rows = [packed] + [along(packed, step) for step in range(1, outer)]
    rows = rows + [other_core(block) for block in rows]
    dq_own, dq_other, dpair, *dpairs = attend(rows, pairs, heads, groups, score_scale)
    for send, part in zip(sends, dpairs):
        dpair = dpair + f32(send(part))
    dq = (dq_own + f32(other_core(dq_other))).reshape(outer, own_rows, width)
    total = dq[0]
    for step in range(1, outer):
        total = total + f32(along(bf16(dq[step]), outer - step))
    total = bf16(total)
    group_width = width // groups
    swapped = jnp.concatenate([total[:, group_width:], total[:, :group_width]], axis=1)
    grad_queries = jnp.where(lax.axis_index("kv") == 0, total, swapped)
    return grad_queries, bf16(dpair[:, :head_width]), bf16(dpair[:, head_width:])


def head_columns(block, first, width):
    return lax.dynamic_slice_in_dim(block, first, width, 1)


def seq_major(block, kv_count, seq_count):
    total_rows = block.shape[0]
    width = block.shape[1]
    shaped = block.reshape(kv_count, seq_count, total_rows // (kv_count * seq_count), width)
    return shaped.transpose(1, 0, 2, 3).reshape(total_rows, width)


def make_accumulate(
    lse_group,
    delta_group,
    group_index,
    group_width,
    group_heads,
    head_width,
    score_scale,
    video_keys,
    video_values,
):

    def accumulate(totals, pieces, offset):
        key_total, value_total, query_rows = totals
        query_block, grad_block = pieces
        query_block = head_columns(query_block, group_index * group_width, group_width)
        grad_block = head_columns(grad_block, group_index * group_width, group_width)
        columns = []
        for member in range(group_heads):
            query_head = query_block[:, member * head_width : (member + 1) * head_width]
            grad_head = grad_block[:, member * head_width : (member + 1) * head_width]
            scores = (
                jnp.einsum("nd,kd->nk", query_head, video_keys, preferred_element_type=jnp.float32)
                * score_scale
            )
            probs = jnp.exp(scores - lse_group[:, member : member + 1])
            probs_half = probs.astype(jnp.bfloat16)
            value_total = value_total + jnp.einsum(
                "nk,nd->kd", probs_half, grad_head, preferred_element_type=jnp.float32
            )
            dprobs = jnp.einsum(
                "nd,kd->nk", grad_head, video_values, preferred_element_type=jnp.float32
            )
            dscores = (probs * (dprobs - delta_group[:, member : member + 1])).astype(jnp.bfloat16)
            key_total = key_total + jnp.einsum(
                "nk,nd->kd", dscores, query_head, preferred_element_type=jnp.float32
            )
            columns.append(
                jnp.einsum("nk,kd->nd", dscores, video_keys, preferred_element_type=jnp.float32)
            )
        query_rows = jnp.concatenate(columns, axis=1)
        return (key_total, value_total, query_rows)

    return accumulate


def shards(queries, out_grad, saved_out, saved_lse, video_keys, video_values):
    kv_count = lax.axis_size("kv")
    seq_count = lax.axis_size("seq")
    group_index = lax.axis_index("kv")
    head_width = video_keys.shape[1]
    group_heads = saved_lse.shape[1] // kv_count
    group_width = group_heads * head_width
    own_rows = queries.shape[0]
    total_rows = own_rows * kv_count * seq_count
    score_scale = 1.0 / math.sqrt(head_width)
    products = out_grad.astype(jnp.float32) * saved_out.astype(jnp.float32)
    own_delta = products.reshape(own_rows, -1, head_width).sum(axis=2)
    lse_all, delta_all = (
        lax.all_gather(saved_lse, ("kv", "seq"), axis=0, tiled=True),
        lax.all_gather(own_delta, ("kv", "seq"), axis=0, tiled=True),
    )
    lse_wide = head_columns(lse_all, group_index * group_heads, group_heads)
    delta_wide = head_columns(delta_all, group_index * group_heads, group_heads)
    key_rows = video_keys.shape[0]
    initial = (
        jnp.zeros((key_rows, head_width), jnp.float32),
        jnp.zeros((key_rows, head_width), jnp.float32),
        jnp.zeros((total_rows, group_width), jnp.float32),
    )
    wide_step = make_accumulate(
        lse_wide,
        delta_wide,
        group_index,
        group_width,
        group_heads,
        head_width,
        score_scale,
        video_keys,
        video_values,
    )
    gathered = (
        lax.all_gather(queries, ("kv", "seq"), axis=0, tiled=True),
        lax.all_gather(out_grad, ("kv", "seq"), axis=0, tiled=True),
    )
    key_total, value_total, query_rows = wide_step(initial, gathered, 0)
    query_rows = seq_major(query_rows, kv_count, seq_count)
    summed = lax.psum_scatter(
        query_rows.reshape(seq_count, total_rows // seq_count, group_width),
        "seq",
        scatter_dimension=0,
        tiled=True,
    )
    rounded = (summed * score_scale).astype(jnp.bfloat16).reshape(kv_count, own_rows, group_width)
    returned = lax.all_to_all(rounded, "kv", split_axis=0, concat_axis=2, tiled=True)
    grad_queries = returned.reshape(own_rows, kv_count * group_width)
    return (
        grad_queries,
        (key_total * score_scale).astype(jnp.bfloat16),
        value_total.astype(jnp.bfloat16),
    )


def fits_planes(kv_count, seq_count, args):
    queries, _, _, saved_lse, video_keys, _ = args
    return (
        kv_count == 2
        and seq_count % 4 == 0
        and queries.shape[0] % 16 == 0
        and video_keys.shape[0] % 16 == 0
        and video_keys.shape[1] == LANES
        and 2 * PIECES * saved_lse.shape[1] <= LANES
    )


def program(*args):
    if fits_planes(lax.axis_size("kv"), lax.axis_size("seq"), args):
        return planes(*args)
    return shards(*args)


def solution(mesh):
    return jax.shard_map(
        program,
        mesh=mesh,
        in_specs=(
            P(("kv", "seq"), None),
            P(("kv", "seq"), None),
            P(("kv", "seq"), None),
            P(("kv", "seq"), None),
            P("seq", "kv"),
            P("seq", "kv"),
        ),
        out_specs=(P(("kv", "seq"), None), P("seq", "kv"), P("seq", "kv")),
        check_vma=False,
    )
```

```python
import functools
import math

import jax
import jax.numpy as jnp
from jax import lax
from jax.experimental import pallas as pl
from jax.experimental.pallas import tpu as pltpu
from jax.sharding import PartitionSpec as P

LANES = 128
PIECES = 3
VMEM_BYTES = 32 * 1024 * 1024


def vmem(count):
    return [pl.BlockSpec(memory_space=pltpu.VMEM)] * count


def bf16(value):
    return value.astype(jnp.bfloat16)


def f32(value):
    return value.astype(jnp.float32)


def load_kernel(
    heads, groups,
    queries, out_grad, saved_out, saved_lse, keys, values,
    rows_out, pairs_out, saved_block, lse_block, done,
):
    width = queries.shape[1]
    group_width = width // groups
    head_width = width // heads
    group = lax.axis_index("kv")
    moves = [
        (keys, pairs_out.at[:, pl.ds(0, head_width)]),
        (values, pairs_out.at[:, pl.ds(head_width, head_width)]),
        (saved_lse, lse_block),
    ]
    for step in range(groups):
        source = lax.rem(group + step, groups)
        columns = pl.ds(pl.multiple_of(source * group_width, group_width), group_width)
        target = step * group_width
        moves.append((out_grad.at[:, columns], rows_out.at[:, pl.ds(width + target, group_width)]))
        moves.append((saved_out.at[:, columns], saved_block.at[:, pl.ds(target, group_width)]))
        moves.append((queries.at[:, columns], rows_out.at[:, pl.ds(target, group_width)]))
    copies = [
        pltpu.make_async_copy(source, target, done.at[index])
        for index, (source, target) in enumerate(moves)
    ]
    for copy in copies:
        copy.start()
    rows_out[:, 2 * width :] = jnp.zeros((rows_out.shape[0], LANES), jnp.bfloat16)
    for copy in copies:
        copy.wait()


def load(queries, out_grad, saved_out, saved_lse, keys, values, groups):
    own_rows, width = queries.shape
    heads = saved_lse.shape[0]
    return pl.pallas_call(
        functools.partial(load_kernel, heads, groups),
        out_shape=(
            jax.ShapeDtypeStruct((own_rows, 2 * width + LANES), jnp.bfloat16),
            jax.ShapeDtypeStruct((keys.shape[0], 2 * keys.shape[1]), jnp.bfloat16),
            jax.ShapeDtypeStruct((own_rows, width), jnp.bfloat16),
            jax.ShapeDtypeStruct(saved_lse.shape, jnp.float32),
        ),
        in_specs=[pl.BlockSpec(memory_space=pltpu.HBM)] * 6,
        out_specs=tuple(vmem(4)),
        scratch_shapes=[pltpu.SemaphoreType.DMA((3 * groups + 3,))],
        compiler_params=pltpu.CompilerParams(vmem_limit_bytes=VMEM_BYTES),
    )(*[
        pltpu.with_memory_space_constraint(array, pltpu.HBM)
        for array in (queries, out_grad, saved_out, saved_lse, keys, values)
    ])


def stats_kernel(heads, groups, score_scale, rows_in, saved_block, lse_block, rows_out):
    own_rows, width = saved_block.shape
    group_heads = heads // groups
    head_width = width // heads
    group = lax.axis_index("kv")
    rows_out[:, : 2 * width] = rows_in[:, : 2 * width]
    lane = lax.broadcasted_iota(jnp.int32, (own_rows, LANES), 1)
    stats = jnp.zeros((own_rows, LANES), jnp.float32)
    shifts = jnp.concatenate(
        [lse_block[...], jnp.zeros((heads, LANES - own_rows), jnp.float32)], axis=1
    ).T[:own_rows] * (1.0 / score_scale)
    for head in range(heads):
        columns = slice(head * head_width, (head + 1) * head_width)
        grad_columns = slice(width + head * head_width, width + (head + 1) * head_width)
        products = f32(rows_in[:, grad_columns]) * f32(saved_block[:, columns])
        delta = jnp.sum(products, axis=1, keepdims=True)
        place = (heads + head) * PIECES
        stats = jnp.where((lane >= place) & (lane < place + PIECES), delta, stats)
        place = lax.rem(head - group * group_heads + heads, heads) * PIECES
        stats = jnp.where((lane >= place) & (lane < place + PIECES), shifts[:, head : head + 1], stats)
    piece = lax.rem(lane, PIECES)
    first = f32(bf16(stats))
    second = f32(bf16(stats - first))
    third = stats - first - second
    rows_out[:, 2 * width :] = bf16(jnp.where(piece == 0, first, jnp.where(piece == 1, second, third)))


def add_stats(rows, saved_block, lse_block, groups, score_scale):
    heads = lse_block.shape[0]
    return pl.pallas_call(
        functools.partial(stats_kernel, heads, groups, score_scale),
        out_shape=jax.ShapeDtypeStruct(rows.shape, rows.dtype),
        in_specs=vmem(3),
        out_specs=vmem(1)[0],
        compiler_params=pltpu.CompilerParams(vmem_limit_bytes=VMEM_BYTES),
        cost_estimate=pl.CostEstimate(flops=2000, bytes_accessed=0, transcendentals=0),
    )(rows, saved_block, lse_block)


def dot(left, right, left_dim, right_dim):
    return lax.dot_general(
        left, right, (((left_dim,), (right_dim,)), ((), ())), preferred_element_type=jnp.float32
    )


def attend_kernel(heads, groups, score_scale, arrays, order, members, carried, last, *refs):
    refs = list(refs)
    held = [refs.pop(0) for _ in range(arrays)]
    pairs = [refs.pop(0) for _ in members]
    before = refs.pop(0) if carried else None
    dq_outs = [refs.pop(0) for _ in range(2 if last else 1)]
    dpairs = refs
    block_rows = held[0].shape[0]
    width = (held[0].shape[1] - LANES) // 2
    head_width = width // heads
    group_heads = heads // groups
    all_rows = len(order) * block_rows
    rows = [held[array].at[pl.ds(place * block_rows, block_rows)] for array, place in order]
    half = all_rows // 2
    key_rows = pairs[0].shape[0]
    exponent = score_scale * math.log2(math.e)
    lane = lax.broadcasted_iota(jnp.int32, (all_rows, LANES), 1)
    stats = jnp.concatenate([block[:, 2 * width :] for block in rows], axis=0)
    none = jnp.zeros_like(stats)
    minus = jnp.full((key_rows, LANES), -1.0, jnp.bfloat16)

    def stacked(start):
        return jnp.concatenate(
            [
                block[:, start + member * head_width : start + (member + 1) * head_width]
                for member in range(group_heads)
                for block in rows
            ],
            axis=0,
        )

    def picked(first):
        firsts = [first + member * PIECES for member in range(group_heads)]
        return jnp.concatenate(
            [jnp.where((lane >= place) & (lane < place + PIECES), stats, none) for place in firsts], axis=0
        )

    for group in sorted(set(members)):
        head = group * group_heads
        query = stacked(head * head_width)
        grad = stacked(width + head * head_width)
        query_wide = jnp.concatenate([query, picked(head * PIECES)], axis=1)
        grad_wide = jnp.concatenate([grad, picked((heads + head) * PIECES)], axis=1)
        columns = slice(head * all_rows, (head + group_heads) * all_rows)
        dquery = before[:, columns] if carried else None
        for index, member in enumerate(members):
            if member != group:
                continue
            keys = pairs[index][:, :head_width]
            values = pairs[index][:, head_width:]
            scores = dot(jnp.concatenate([keys, minus], axis=1), query_wide, 1, 1)
            probs = jnp.exp2(scores * exponent)
            dprobs = dot(jnp.concatenate([values, minus], axis=1), grad_wide, 1, 1)
            dscores = bf16(probs * dprobs)
            out = dpairs[index]
            out[:, head_width:] = dot(bf16(probs), grad, 1, 0).astype(out.dtype)
            out[:, :head_width] = (dot(dscores, query, 1, 0) * score_scale).astype(out.dtype)
            term = dot(keys, dscores, 0, 0)
            dquery = term if dquery is None else dquery + term
        if not last:
            if dquery is not None:
                dq_outs[0][:, columns] = dquery
            continue
        for member in range(group_heads):
            part = dquery[:, member * all_rows : (member + 1) * all_rows].T * score_scale
            columns = slice((head + member) * head_width, (head + member + 1) * head_width)
            dq_outs[0][:, columns] = part[:half]
            dq_outs[1][:, columns] = bf16(part[half:])
    missing = sorted(set(range(groups)) - set(members))
    for group in missing:
        columns = slice(group * group_heads * all_rows, (group + 1) * group_heads * all_rows)
        kept = before[:, columns] if carried else jnp.zeros((head_width, group_heads * all_rows), jnp.float32)
        if not last:
            dq_outs[0][:, columns] = kept
            continue
        for member in range(group_heads):
            part = kept[:, member * all_rows : (member + 1) * all_rows].T * score_scale
            head = group * group_heads + member
            columns = slice(head * head_width, (head + 1) * head_width)
            dq_outs[0][:, columns] = part[:half]
            dq_outs[1][:, columns] = bf16(part[half:])


def attend(rows, order, pairs, members, kinds, before, last, heads, groups, score_scale):
    block_rows, packed = rows[0].shape
    width = (packed - LANES) // 2
    all_rows = len(order) * block_rows
    key_rows, head_width = pairs[0].shape[0], pairs[0].shape[1] // 2
    if last:
        outs = [
            jax.ShapeDtypeStruct((all_rows // 2, width), jnp.float32),
            jax.ShapeDtypeStruct((all_rows // 2, width), jnp.bfloat16),
        ]
    else:
        outs = [jax.ShapeDtypeStruct((head_width, heads * all_rows), jnp.float32)]
    outs = outs + [jax.ShapeDtypeStruct(pairs[0].shape, kind) for kind in kinds]
    operands = list(rows) + list(pairs) + ([] if before is None else [before])
    products = len(pairs) * key_rows * (heads // groups) * all_rows
    return pl.pallas_call(
        functools.partial(
            attend_kernel, heads, groups, score_scale, len(rows), order, members, before is not None, last
        ),
        out_shape=tuple(outs),
        in_specs=vmem(len(operands)),
        out_specs=tuple(vmem(len(outs))),
        compiler_params=pltpu.CompilerParams(vmem_limit_bytes=VMEM_BYTES),
        cost_estimate=pl.CostEstimate(
            flops=10 * products * head_width, bytes_accessed=0, transcendentals=products
        ),
    )(*operands)


def turn_seq(array, seq_count, target):
    return lax.ppermute(array, "seq", [(place, target(place)) for place in range(seq_count)])


def planes(queries, out_grad, saved_out, saved_lse, video_keys, video_values):
    groups = lax.axis_size("kv")
    seq_count = lax.axis_size("seq")
    own_rows, width = queries.shape
    heads = saved_lse.shape[1]
    head_width = video_keys.shape[1]
    score_scale = 1.0 / math.sqrt(head_width)

    def near(array):
        return turn_seq(array, seq_count, lambda place: place ^ (8 if place % 2 else 4))

    def other_near(array):
        return turn_seq(array, seq_count, lambda place: place ^ (4 if place % 2 else 8))

    def far(array):
        return turn_seq(array, seq_count, lambda place: place ^ 12)

    def other_core(array):
        return turn_seq(array, seq_count, lambda place: place ^ 1)

    def middle(array):
        return turn_seq(array, seq_count, lambda place: place ^ 2)

    def across(array):
        return lax.ppermute(array, "kv", [(0, 1), (1, 0)])

    def diagonal(array):
        steps = [
            (kv * seq_count + place, (1 - kv) * seq_count + (place ^ 2))
            for kv in range(2)
            for place in range(seq_count)
        ]
        return lax.ppermute(array, ("kv", "seq"), steps)

    rows, pair, saved_block, lse_block = load(
        queries, out_grad, saved_out, saved_lse.T, video_keys, video_values, groups
    )
    packed = add_stats(rows, saved_block, lse_block, groups, score_scale)
    pair_across, pair_middle = across(pair), middle(pair)
    keys_far = middle(pair_across[:, :head_width])
    values_far = across(pair_middle[:, head_width:])
    pairs = [pair, pair_middle, pair_across, jnp.concatenate([keys_far, values_far], axis=1)]
    beside = other_core(packed)
    from_far = far(packed)
    from_near = near(jnp.concatenate([packed, beside], axis=0))
    rows = [packed, beside, from_near, other_core(from_near), from_far, other_core(from_far)]
    order = ((0, 0), (2, 0), (3, 1), (4, 0), (1, 0), (3, 0), (2, 1), (5, 0))
    sends = (middle, across, diagonal)
    dq = None
    dpairs = []
    calls = ((0, 1, 2, 3),)
    for call in calls:
        last = call is calls[-1]
        found = attend(
            rows,
            order,
            [pairs[index] for index in call],
            tuple(index // 2 for index in call),
            [jnp.float32 if index == 0 else jnp.bfloat16 for index in call],
            dq,
            last,
            heads,
            groups,
            score_scale,
        )
        if last:
            dq_own, dq_other, *parts = found
        else:
            dq, *parts = found
        dpairs += list(zip(call, parts))
    dpair, *dpairs = [part for _, part in sorted(dpairs, key=lambda item: item[0])]
    for send, part in zip(sends, dpairs):
        dpair = dpair + f32(send(part))
    dq = (dq_own + f32(other_core(dq_other))).reshape(-1, own_rows, width)
    total = dq[0]
    for place, send in ((3, far), (2, other_near), (1, near)):
        total = total + f32(send(bf16(dq[place])))
    total = bf16(total)
    group_width = width // groups
    swapped = jnp.concatenate([total[:, group_width:], total[:, :group_width]], axis=1)
    grad_queries = jnp.where(lax.axis_index("kv") == 0, total, swapped)
    return grad_queries, bf16(dpair[:, :head_width]), bf16(dpair[:, head_width:])


def head_columns(block, first, width):
    return lax.dynamic_slice_in_dim(block, first, width, 1)


def seq_major(block, kv_count, seq_count):
    total_rows = block.shape[0]
    width = block.shape[1]
    shaped = block.reshape(kv_count, seq_count, total_rows // (kv_count * seq_count), width)
    return shaped.transpose(1, 0, 2, 3).reshape(total_rows, width)


def make_accumulate(
    lse_group,
    delta_group,
    group_index,
    group_width,
    group_heads,
    head_width,
    score_scale,
    video_keys,
    video_values,
):

    def accumulate(totals, pieces, offset):
        key_total, value_total, query_rows = totals
        query_block, grad_block = pieces
        query_block = head_columns(query_block, group_index * group_width, group_width)
        grad_block = head_columns(grad_block, group_index * group_width, group_width)
        columns = []
        for member in range(group_heads):
            query_head = query_block[:, member * head_width : (member + 1) * head_width]
            grad_head = grad_block[:, member * head_width : (member + 1) * head_width]
            scores = (
                jnp.einsum("nd,kd->nk", query_head, video_keys, preferred_element_type=jnp.float32)
                * score_scale
            )
            probs = jnp.exp(scores - lse_group[:, member : member + 1])
            probs_half = probs.astype(jnp.bfloat16)
            value_total = value_total + jnp.einsum(
                "nk,nd->kd", probs_half, grad_head, preferred_element_type=jnp.float32
            )
            dprobs = jnp.einsum(
                "nd,kd->nk", grad_head, video_values, preferred_element_type=jnp.float32
            )
            dscores = (probs * (dprobs - delta_group[:, member : member + 1])).astype(jnp.bfloat16)
            key_total = key_total + jnp.einsum(
                "nk,nd->kd", dscores, query_head, preferred_element_type=jnp.float32
            )
            columns.append(
                jnp.einsum("nk,kd->nd", dscores, video_keys, preferred_element_type=jnp.float32)
            )
        query_rows = jnp.concatenate(columns, axis=1)
        return (key_total, value_total, query_rows)

    return accumulate


def shards(queries, out_grad, saved_out, saved_lse, video_keys, video_values):
    kv_count = lax.axis_size("kv")
    seq_count = lax.axis_size("seq")
    group_index = lax.axis_index("kv")
    head_width = video_keys.shape[1]
    group_heads = saved_lse.shape[1] // kv_count
    group_width = group_heads * head_width
    own_rows = queries.shape[0]
    total_rows = own_rows * kv_count * seq_count
    score_scale = 1.0 / math.sqrt(head_width)
    products = out_grad.astype(jnp.float32) * saved_out.astype(jnp.float32)
    own_delta = products.reshape(own_rows, -1, head_width).sum(axis=2)
    lse_all, delta_all = (
        lax.all_gather(saved_lse, ("kv", "seq"), axis=0, tiled=True),
        lax.all_gather(own_delta, ("kv", "seq"), axis=0, tiled=True),
    )
    lse_wide = head_columns(lse_all, group_index * group_heads, group_heads)
    delta_wide = head_columns(delta_all, group_index * group_heads, group_heads)
    key_rows = video_keys.shape[0]
    initial = (
        jnp.zeros((key_rows, head_width), jnp.float32),
        jnp.zeros((key_rows, head_width), jnp.float32),
        jnp.zeros((total_rows, group_width), jnp.float32),
    )
    wide_step = make_accumulate(
        lse_wide,
        delta_wide,
        group_index,
        group_width,
        group_heads,
        head_width,
        score_scale,
        video_keys,
        video_values,
    )
    gathered = (
        lax.all_gather(queries, ("kv", "seq"), axis=0, tiled=True),
        lax.all_gather(out_grad, ("kv", "seq"), axis=0, tiled=True),
    )
    key_total, value_total, query_rows = wide_step(initial, gathered, 0)
    query_rows = seq_major(query_rows, kv_count, seq_count)
    summed = lax.psum_scatter(
        query_rows.reshape(seq_count, total_rows // seq_count, group_width),
        "seq",
        scatter_dimension=0,
        tiled=True,
    )
    rounded = (summed * score_scale).astype(jnp.bfloat16).reshape(kv_count, own_rows, group_width)
    returned = lax.all_to_all(rounded, "kv", split_axis=0, concat_axis=2, tiled=True)
    grad_queries = returned.reshape(own_rows, kv_count * group_width)
    return (
        grad_queries,
        (key_total * score_scale).astype(jnp.bfloat16),
        value_total.astype(jnp.bfloat16),
    )


def fits_planes(kv_count, seq_count, args):
    queries, _, _, saved_lse, video_keys, _ = args
    return (
        kv_count == 2
        and seq_count == 16
        and queries.shape[0] % 16 == 0
        and video_keys.shape[0] % 16 == 0
        and video_keys.shape[1] == LANES
        and 2 * PIECES * saved_lse.shape[1] <= LANES
    )


def program(*args):
    if fits_planes(lax.axis_size("kv"), lax.axis_size("seq"), args):
        return planes(*args)
    return shards(*args)


def solution(mesh):
    return jax.shard_map(
        program,
        mesh=mesh,
        in_specs=(
            P(("kv", "seq"), None),
            P(("kv", "seq"), None),
            P(("kv", "seq"), None),
            P(("kv", "seq"), None),
            P("seq", "kv"),
            P("seq", "kv"),
        ),
        out_specs=(P(("kv", "seq"), None), P("seq", "kv"), P("seq", "kv")),
        check_vma=False,
    )
```

```python
import functools
import math

import jax
import jax.numpy as jnp
from jax import lax
from jax.experimental import pallas as pl
from jax.experimental.pallas import tpu as pltpu
from jax.sharding import PartitionSpec as P

LANES = 128
PIECES = 3
VMEM_BYTES = 32 * 1024 * 1024


def vmem(count):
    return [pl.BlockSpec(memory_space=pltpu.VMEM)] * count


def bf16(value):
    return value.astype(jnp.bfloat16)


def f32(value):
    return value.astype(jnp.float32)


def pack_kernel(
    heads, groups, score_scale,
    queries, out_grad, saved_out, saved_lse, keys, values,
    rows_out, pairs_out, saved_block, lse_block, done,
):
    own_rows, width = queries.shape
    group_width = width // groups
    group_heads = heads // groups
    head_width = width // heads
    group = lax.axis_index("kv")
    moves = [(saved_lse, lse_block)]
    for step in range(groups):
        source = lax.rem(group + step, groups)
        columns = pl.ds(pl.multiple_of(source * group_width, group_width), group_width)
        target = step * group_width
        moves.append((out_grad.at[:, columns], rows_out.at[:, pl.ds(width + target, group_width)]))
        moves.append((saved_out.at[:, columns], saved_block.at[:, pl.ds(target, group_width)]))
    needed = len(moves)
    for step in range(groups):
        source = lax.rem(group + step, groups)
        columns = pl.ds(pl.multiple_of(source * group_width, group_width), group_width)
        moves.append((queries.at[:, columns], rows_out.at[:, pl.ds(step * group_width, group_width)]))
    moves.append((keys, pairs_out.at[:, pl.ds(0, head_width)]))
    moves.append((values, pairs_out.at[:, pl.ds(head_width, head_width)]))
    copies = [
        pltpu.make_async_copy(source, target, done.at[index])
        for index, (source, target) in enumerate(moves)
    ]
    for copy in copies:
        copy.start()
    lane = lax.broadcasted_iota(jnp.int32, (own_rows, LANES), 1)
    piece = lax.rem(lane, PIECES)
    stats = jnp.zeros((own_rows, LANES), jnp.float32)
    for copy in copies[:needed]:
        copy.wait()
    shifts = jnp.concatenate(
        [lse_block[...], jnp.zeros((heads, LANES - own_rows), jnp.float32)], axis=1
    ).T[:own_rows] * (1.0 / score_scale)
    for head in range(heads):
        columns = slice(head * head_width, (head + 1) * head_width)
        grad_columns = slice(width + head * head_width, width + (head + 1) * head_width)
        products = f32(rows_out[:, grad_columns]) * f32(saved_block[:, columns])
        delta = jnp.sum(products, axis=1, keepdims=True)
        place = (heads + head) * PIECES
        stats = jnp.where((lane >= place) & (lane < place + PIECES), delta, stats)
        place = lax.rem(head - group * group_heads + heads, heads) * PIECES
        stats = jnp.where((lane >= place) & (lane < place + PIECES), shifts[:, head : head + 1], stats)
    first = f32(bf16(stats))
    second = f32(bf16(stats - first))
    third = stats - first - second
    rows_out[:, 2 * width :] = bf16(jnp.where(piece == 0, first, jnp.where(piece == 1, second, third)))
    for copy in copies[needed:]:
        copy.wait()


def pack(queries, out_grad, saved_out, saved_lse, keys, values, groups, score_scale):
    own_rows, width = queries.shape
    heads = saved_lse.shape[0]
    return pl.pallas_call(
        functools.partial(pack_kernel, heads, groups, score_scale),
        out_shape=(
            jax.ShapeDtypeStruct((own_rows, 2 * width + LANES), jnp.bfloat16),
            jax.ShapeDtypeStruct((keys.shape[0], 2 * keys.shape[1]), jnp.bfloat16),
        ),
        in_specs=[pl.BlockSpec(memory_space=pltpu.HBM)] * 6,
        out_specs=tuple(vmem(2)),
        scratch_shapes=[
            pltpu.VMEM((own_rows, width), jnp.bfloat16),
            pltpu.VMEM(saved_lse.shape, jnp.float32),
            pltpu.SemaphoreType.DMA((3 * groups + 3,)),
        ],
        compiler_params=pltpu.CompilerParams(vmem_limit_bytes=VMEM_BYTES),
    )(*[
        pltpu.with_memory_space_constraint(array, pltpu.HBM)
        for array in (queries, out_grad, saved_out, saved_lse, keys, values)
    ])


def dot(left, right, left_dim, right_dim):
    return lax.dot_general(
        left, right, (((left_dim,), (right_dim,)), ((), ())), preferred_element_type=jnp.float32
    )


def attend_kernel(heads, groups, score_scale, arrays, order, pair_count, carried, *refs):
    refs = list(refs)
    held = [refs.pop(0) for _ in range(arrays)]
    pairs = [refs.pop(0) for _ in range(pair_count)]
    before = [refs.pop(0) for _ in range(pair_count)] if carried else None
    dq_own, dq_other, *dpairs = refs
    block_rows = held[0].shape[0]
    width = (held[0].shape[1] - LANES) // 2
    head_width = width // heads
    group_heads = heads // groups
    all_rows = len(order) * block_rows
    half = all_rows // 2
    rows = [held[array].at[pl.ds(place * block_rows, block_rows)] for array, place in order]
    key_rows = pairs[0].shape[0]
    per_group = pair_count // groups
    exponent = score_scale * math.log2(math.e)
    lane = lax.broadcasted_iota(jnp.int32, (all_rows, LANES), 1)
    stats = jnp.concatenate([block[:, 2 * width :] for block in rows], axis=0)
    none = jnp.zeros_like(stats)

    def stacked(start):
        return jnp.concatenate(
            [
                block[:, start + member * head_width : start + (member + 1) * head_width]
                for member in range(group_heads)
                for block in rows
            ],
            axis=0,
        )

    def picked(first):
        firsts = [first + member * PIECES for member in range(group_heads)]
        return jnp.concatenate(
            [jnp.where((lane >= place) & (lane < place + PIECES), stats, none) for place in firsts], axis=0
        )

    for group in range(groups):
        head = group * group_heads
        query = stacked(head * head_width)
        grad = stacked(width + head * head_width)
        query_wide = jnp.concatenate([query, picked(head * PIECES)], axis=1)
        grad_wide = jnp.concatenate([grad, picked((heads + head) * PIECES)], axis=1)
        members = range(group * per_group, (group + 1) * per_group)
        keys = jnp.concatenate([pairs[index][:, :head_width] for index in members], axis=0)
        values = jnp.concatenate([pairs[index][:, head_width:] for index in members], axis=0)
        minus = jnp.full(keys.shape, -1.0, jnp.bfloat16)
        scores = dot(jnp.concatenate([keys, minus], axis=1), query_wide, 1, 1)
        probs = jnp.exp2(scores * exponent)
        dprobs = dot(jnp.concatenate([values, minus], axis=1), grad_wide, 1, 1)
        dscores = bf16(probs * dprobs)
        dvalues = dot(bf16(probs), grad, 1, 0)
        dkeys = dot(dscores, query, 1, 0) * score_scale
        for place, index in enumerate(members):
            out = dpairs[index]
            taken = slice(place * key_rows, (place + 1) * key_rows)
            dkey, dvalue = dkeys[taken], dvalues[taken]
            if carried:
                dkey = dkey + before[index][:, :head_width]
                dvalue = dvalue + before[index][:, head_width:]
            out[:, :head_width] = dkey.astype(out.dtype)
            out[:, head_width:] = dvalue.astype(out.dtype)
        dquery = dot(keys, dscores, 0, 0).T * score_scale
        for member in range(group_heads):
            part = dquery[member * all_rows : (member + 1) * all_rows]
            columns = slice((head + member) * head_width, (head + member + 1) * head_width)
            dq_own[:, columns] = part[:half]
            dq_other[:, columns] = bf16(part[half:])


def attend(rows, order, pairs, before, kinds, heads, groups, score_scale):
    block_rows, packed = rows[0].shape
    width = (packed - LANES) // 2
    half = len(order) // 2 * block_rows
    key_rows, head_width = pairs[0].shape[0], pairs[0].shape[1] // 2
    outs = [
        jax.ShapeDtypeStruct((half, width), jnp.float32),
        jax.ShapeDtypeStruct((half, width), jnp.bfloat16),
    ] + [jax.ShapeDtypeStruct(pairs[0].shape, kind) for kind in kinds]
    operands = list(rows) + list(pairs) + list(before)
    products = len(pairs) * key_rows * (heads // groups) * 2 * half
    return pl.pallas_call(
        functools.partial(
            attend_kernel, heads, groups, score_scale, len(rows), order, len(pairs), bool(before)
        ),
        out_shape=tuple(outs),
        in_specs=vmem(len(operands)),
        out_specs=tuple(vmem(len(outs))),
        compiler_params=pltpu.CompilerParams(vmem_limit_bytes=VMEM_BYTES),
        cost_estimate=pl.CostEstimate(
            flops=10 * products * head_width, bytes_accessed=0, transcendentals=products
        ),
    )(*operands)


def finish_kernel(groups, terms, *refs):
    query_terms, pair_terms = refs[:terms], refs[terms : 2 * terms]
    grad_queries, grad_keys, grad_values, queries_block, keys_block, values_block, done = refs[2 * terms :]
    group = lax.axis_index("kv")
    group_width = queries_block.shape[1] // groups
    head_width = keys_block.shape[1]

    def total(parts, columns):
        return functools.reduce(lambda left, right: left + right, [f32(part[:, columns]) for part in parts])

    copies = []
    for block, target, columns in (
        (keys_block, grad_keys, slice(0, head_width)),
        (values_block, grad_values, slice(head_width, 2 * head_width)),
    ):
        block[...] = bf16(total(pair_terms, columns))
        copies.append(pltpu.make_async_copy(block, target, done.at[len(copies)]))
        copies[-1].start()
    for step in range(groups):
        columns = slice(step * group_width, (step + 1) * group_width)
        queries_block[:, columns] = bf16(total(query_terms, columns))
        target = lax.rem(group + step, groups) * group_width
        target = grad_queries.at[:, pl.ds(pl.multiple_of(target, group_width), group_width)]
        source = queries_block.at[:, pl.ds(step * group_width, group_width)]
        copies.append(pltpu.make_async_copy(source, target, done.at[len(copies)]))
        copies[-1].start()
    for copy in copies:
        copy.wait()


def finish(query_terms, pair_terms, groups):
    own_rows, width = query_terms[0].shape
    key_rows, head_width = pair_terms[0].shape[0], pair_terms[0].shape[1] // 2
    shapes = ((own_rows, width), (key_rows, head_width), (key_rows, head_width))
    operands = list(query_terms) + list(pair_terms)
    return pl.pallas_call(
        functools.partial(finish_kernel, groups, len(query_terms)),
        out_shape=tuple(pltpu.HBM(shape, jnp.bfloat16) for shape in shapes),
        in_specs=vmem(len(operands)),
        out_specs=tuple([pl.BlockSpec(memory_space=pltpu.HBM)] * 3),
        scratch_shapes=[pltpu.VMEM(shape, jnp.bfloat16) for shape in shapes]
        + [pltpu.SemaphoreType.DMA((groups + 2,))],
        compiler_params=pltpu.CompilerParams(vmem_limit_bytes=VMEM_BYTES),
    )(*operands)


def turn_seq(array, seq_count, target):
    return lax.ppermute(array, "seq", [(place, target(place)) for place in range(seq_count)])


def planes(queries, out_grad, saved_out, saved_lse, video_keys, video_values):
    groups = lax.axis_size("kv")
    seq_count = lax.axis_size("seq")
    own_rows, width = queries.shape
    heads = saved_lse.shape[1]
    head_width = video_keys.shape[1]
    score_scale = 1.0 / math.sqrt(head_width)

    def steps(array, even, odd):
        return turn_seq(array, seq_count, lambda place: place ^ (4 * (odd if place % 2 else even)))

    def other_core(array):
        return turn_seq(array, seq_count, lambda place: place ^ 1)

    def middle(array):
        return turn_seq(array, seq_count, lambda place: place ^ 2)

    def across(array):
        return lax.ppermute(array, "kv", [(0, 1), (1, 0)])

    def diagonal(array):
        steps = [
            (kv * seq_count + place, (1 - kv) * seq_count + (place ^ 2))
            for kv in range(2)
            for place in range(seq_count)
        ]
        return lax.ppermute(array, ("kv", "seq"), steps)

    packed, pair = pack(
        queries, out_grad, saved_out, saved_lse.T, video_keys, video_values, groups, score_scale
    )
    pair_across, pair_middle = across(pair), middle(pair)
    keys_far = middle(pair_across[:, :head_width])
    values_far = across(pair_middle[:, head_width:])
    pairs = [pair, pair_middle, pair_across, jnp.concatenate([keys_far, values_far], axis=1)]
    beside = other_core(packed)
    from_far = steps(packed, 3, 3)
    from_near = steps(jnp.concatenate([packed, beside], axis=0), 1, 2)
    rows = [packed, beside, from_near, other_core(from_near), from_far, other_core(from_far)]
    order = ((0, 0), (2, 0), (3, 1), (4, 0), (1, 0), (3, 0), (2, 1), (5, 0))
    kinds = [jnp.float32] + [jnp.bfloat16] * 3
    dq_own, dq_other, *dpairs = attend(rows, order, pairs, [], kinds, heads, groups, score_scale)
    parts = dpairs[1:]
    pair_terms = [dpairs[0]] + [send(parts[place]) for send, place in ((middle, 0), (across, 1), (diagonal, 2))]
    dq = (dq_own + f32(other_core(dq_other))).reshape(-1, own_rows, width)
    query_terms = [dq[0]] + [
        steps(bf16(dq[place]), even, odd) for place, even, odd in ((1, 1, 2), (2, 2, 1), (3, 3, 3))
    ]
    return finish(query_terms, pair_terms, groups)


def head_columns(block, first, width):
    return lax.dynamic_slice_in_dim(block, first, width, 1)


def seq_major(block, kv_count, seq_count):
    total_rows = block.shape[0]
    width = block.shape[1]
    shaped = block.reshape(kv_count, seq_count, total_rows // (kv_count * seq_count), width)
    return shaped.transpose(1, 0, 2, 3).reshape(total_rows, width)


def make_accumulate(
    lse_group,
    delta_group,
    group_index,
    group_width,
    group_heads,
    head_width,
    score_scale,
    video_keys,
    video_values,
):

    def accumulate(totals, pieces, offset):
        key_total, value_total, query_rows = totals
        query_block, grad_block = pieces
        query_block = head_columns(query_block, group_index * group_width, group_width)
        grad_block = head_columns(grad_block, group_index * group_width, group_width)
        columns = []
        for member in range(group_heads):
            query_head = query_block[:, member * head_width : (member + 1) * head_width]
            grad_head = grad_block[:, member * head_width : (member + 1) * head_width]
            scores = (
                jnp.einsum("nd,kd->nk", query_head, video_keys, preferred_element_type=jnp.float32)
                * score_scale
            )
            probs = jnp.exp(scores - lse_group[:, member : member + 1])
            probs_half = probs.astype(jnp.bfloat16)
            value_total = value_total + jnp.einsum(
                "nk,nd->kd", probs_half, grad_head, preferred_element_type=jnp.float32
            )
            dprobs = jnp.einsum(
                "nd,kd->nk", grad_head, video_values, preferred_element_type=jnp.float32
            )
            dscores = (probs * (dprobs - delta_group[:, member : member + 1])).astype(jnp.bfloat16)
            key_total = key_total + jnp.einsum(
                "nk,nd->kd", dscores, query_head, preferred_element_type=jnp.float32
            )
            columns.append(
                jnp.einsum("nk,kd->nd", dscores, video_keys, preferred_element_type=jnp.float32)
            )
        query_rows = jnp.concatenate(columns, axis=1)
        return (key_total, value_total, query_rows)

    return accumulate


def shards(queries, out_grad, saved_out, saved_lse, video_keys, video_values):
    kv_count = lax.axis_size("kv")
    seq_count = lax.axis_size("seq")
    group_index = lax.axis_index("kv")
    head_width = video_keys.shape[1]
    group_heads = saved_lse.shape[1] // kv_count
    group_width = group_heads * head_width
    own_rows = queries.shape[0]
    total_rows = own_rows * kv_count * seq_count
    score_scale = 1.0 / math.sqrt(head_width)
    products = out_grad.astype(jnp.float32) * saved_out.astype(jnp.float32)
    own_delta = products.reshape(own_rows, -1, head_width).sum(axis=2)
    lse_all, delta_all = (
        lax.all_gather(saved_lse, ("kv", "seq"), axis=0, tiled=True),
        lax.all_gather(own_delta, ("kv", "seq"), axis=0, tiled=True),
    )
    lse_wide = head_columns(lse_all, group_index * group_heads, group_heads)
    delta_wide = head_columns(delta_all, group_index * group_heads, group_heads)
    key_rows = video_keys.shape[0]
    initial = (
        jnp.zeros((key_rows, head_width), jnp.float32),
        jnp.zeros((key_rows, head_width), jnp.float32),
        jnp.zeros((total_rows, group_width), jnp.float32),
    )
    wide_step = make_accumulate(
        lse_wide,
        delta_wide,
        group_index,
        group_width,
        group_heads,
        head_width,
        score_scale,
        video_keys,
        video_values,
    )
    gathered = (
        lax.all_gather(queries, ("kv", "seq"), axis=0, tiled=True),
        lax.all_gather(out_grad, ("kv", "seq"), axis=0, tiled=True),
    )
    key_total, value_total, query_rows = wide_step(initial, gathered, 0)
    query_rows = seq_major(query_rows, kv_count, seq_count)
    summed = lax.psum_scatter(
        query_rows.reshape(seq_count, total_rows // seq_count, group_width),
        "seq",
        scatter_dimension=0,
        tiled=True,
    )
    rounded = (summed * score_scale).astype(jnp.bfloat16).reshape(kv_count, own_rows, group_width)
    returned = lax.all_to_all(rounded, "kv", split_axis=0, concat_axis=2, tiled=True)
    grad_queries = returned.reshape(own_rows, kv_count * group_width)
    return (
        grad_queries,
        (key_total * score_scale).astype(jnp.bfloat16),
        value_total.astype(jnp.bfloat16),
    )


def fits_planes(kv_count, seq_count, args):
    queries, _, _, saved_lse, video_keys, _ = args
    return (
        kv_count == 2
        and seq_count == 16
        and queries.shape[0] % 16 == 0
        and video_keys.shape[0] % 16 == 0
        and video_keys.shape[1] == LANES
        and 2 * PIECES * saved_lse.shape[1] <= LANES
    )


def program(*args):
    if fits_planes(lax.axis_size("kv"), lax.axis_size("seq"), args):
        return planes(*args)
    return shards(*args)


def solution(mesh):
    return jax.shard_map(
        program,
        mesh=mesh,
        in_specs=(
            P(("kv", "seq"), None),
            P(("kv", "seq"), None),
            P(("kv", "seq"), None),
            P(("kv", "seq"), None),
            P("seq", "kv"),
            P("seq", "kv"),
        ),
        out_specs=(P(("kv", "seq"), None), P("seq", "kv"), P("seq", "kv")),
        check_vma=False,
    )
```

```python
import functools
import math

import jax
import jax.numpy as jnp
from jax import lax
from jax.experimental import pallas as pl
from jax.experimental.pallas import tpu as pltpu
from jax.sharding import PartitionSpec as P

LANES = 128
PIECES = 3
VMEM_BYTES = 32 * 1024 * 1024


def vmem(count):
    return [pl.BlockSpec(memory_space=pltpu.VMEM)] * count


def bf16(value):
    return value.astype(jnp.bfloat16)


def f32(value):
    return value.astype(jnp.float32)


def pack_kernel(
    heads, groups, score_scale,
    queries, out_grad, saved_out, saved_lse, keys, values,
    rows_out, pairs_out, saved_block, lse_block, done,
):
    own_rows, width = queries.shape
    group_width = width // groups
    group_heads = heads // groups
    head_width = width // heads
    group = lax.axis_index("kv")
    moves = [(saved_lse, lse_block)]
    for step in range(groups):
        source = lax.rem(group + step, groups)
        columns = pl.ds(pl.multiple_of(source * group_width, group_width), group_width)
        target = step * group_width
        moves.append((out_grad.at[:, columns], rows_out.at[:, pl.ds(width + target, group_width)]))
        moves.append((saved_out.at[:, columns], saved_block.at[:, pl.ds(target, group_width)]))
    needed = len(moves)
    for step in range(groups):
        source = lax.rem(group + step, groups)
        columns = pl.ds(pl.multiple_of(source * group_width, group_width), group_width)
        moves.append((queries.at[:, columns], rows_out.at[:, pl.ds(step * group_width, group_width)]))
    moves.append((keys, pairs_out.at[:, pl.ds(0, head_width)]))
    moves.append((values, pairs_out.at[:, pl.ds(head_width, head_width)]))
    copies = [
        pltpu.make_async_copy(source, target, done.at[index])
        for index, (source, target) in enumerate(moves)
    ]
    for copy in copies:
        copy.start()
    lane = lax.broadcasted_iota(jnp.int32, (own_rows, LANES), 1)
    piece = lax.rem(lane, PIECES)
    stats = jnp.zeros((own_rows, LANES), jnp.float32)
    for copy in copies[:needed]:
        copy.wait()
    shifts = jnp.concatenate(
        [lse_block[...], jnp.zeros((heads, LANES - own_rows), jnp.float32)], axis=1
    ).T[:own_rows] * (1.0 / score_scale)
    for head in range(heads):
        columns = slice(head * head_width, (head + 1) * head_width)
        grad_columns = slice(width + head * head_width, width + (head + 1) * head_width)
        products = f32(rows_out[:, grad_columns]) * f32(saved_block[:, columns])
        delta = jnp.sum(products, axis=1, keepdims=True)
        place = (heads + head) * PIECES
        stats = jnp.where((lane >= place) & (lane < place + PIECES), delta, stats)
        place = lax.rem(head - group * group_heads + heads, heads) * PIECES
        stats = jnp.where((lane >= place) & (lane < place + PIECES), shifts[:, head : head + 1], stats)
    first = f32(bf16(stats))
    second = f32(bf16(stats - first))
    third = stats - first - second
    rows_out[:, 2 * width :] = bf16(jnp.where(piece == 0, first, jnp.where(piece == 1, second, third)))
    for copy in copies[needed:]:
        copy.wait()


def pack(queries, out_grad, saved_out, saved_lse, keys, values, groups, score_scale):
    own_rows, width = queries.shape
    heads = saved_lse.shape[0]
    return pl.pallas_call(
        functools.partial(pack_kernel, heads, groups, score_scale),
        out_shape=(
            jax.ShapeDtypeStruct((own_rows, 2 * width + LANES), jnp.bfloat16),
            jax.ShapeDtypeStruct((keys.shape[0], 2 * keys.shape[1]), jnp.bfloat16),
        ),
        in_specs=[pl.BlockSpec(memory_space=pltpu.HBM)] * 6,
        out_specs=tuple(vmem(2)),
        scratch_shapes=[
            pltpu.VMEM((own_rows, width), jnp.bfloat16),
            pltpu.VMEM(saved_lse.shape, jnp.float32),
            pltpu.SemaphoreType.DMA((3 * groups + 3,)),
        ],
        compiler_params=pltpu.CompilerParams(vmem_limit_bytes=VMEM_BYTES),
    )(*[
        pltpu.with_memory_space_constraint(array, pltpu.HBM)
        for array in (queries, out_grad, saved_out, saved_lse, keys, values)
    ])


def dot(left, right, left_dim, right_dim):
    return lax.dot_general(
        left, right, (((left_dim,), (right_dim,)), ((), ())), preferred_element_type=jnp.float32
    )


def attend_kernel(heads, groups, score_scale, arrays, order, pair_count, carried, *refs):
    refs = list(refs)
    held = [refs.pop(0) for _ in range(arrays)]
    pairs = [refs.pop(0) for _ in range(pair_count)]
    before = [refs.pop(0) for _ in range(pair_count)] if carried else None
    dq_own, dq_other, *dpairs = refs
    block_rows = held[0].shape[0]
    width = (held[0].shape[1] - LANES) // 2
    head_width = width // heads
    group_heads = heads // groups
    all_rows = len(order) * block_rows
    half = all_rows // 2
    rows = [held[array].at[pl.ds(place * block_rows, block_rows)] for array, place in order]
    key_rows = pairs[0].shape[0]
    per_group = pair_count // groups
    exponent = score_scale * math.log2(math.e)
    lane = lax.broadcasted_iota(jnp.int32, (all_rows, LANES), 1)
    stats = jnp.concatenate([block[:, 2 * width :] for block in rows], axis=0)
    none = jnp.zeros_like(stats)

    def stacked(start):
        return jnp.concatenate(
            [
                block[:, start + member * head_width : start + (member + 1) * head_width]
                for member in range(group_heads)
                for block in rows
            ],
            axis=0,
        )

    def picked(first):
        firsts = [first + member * PIECES for member in range(group_heads)]
        return jnp.concatenate(
            [jnp.where((lane >= place) & (lane < place + PIECES), stats, none) for place in firsts], axis=0
        )

    for group in range(groups):
        head = group * group_heads
        query = stacked(head * head_width)
        grad = stacked(width + head * head_width)
        query_wide = jnp.concatenate([query, picked(head * PIECES)], axis=1)
        grad_wide = jnp.concatenate([grad, picked((heads + head) * PIECES)], axis=1)
        members = range(group * per_group, (group + 1) * per_group)
        keys = jnp.concatenate([pairs[index][:, :head_width] for index in members], axis=0)
        values = jnp.concatenate([pairs[index][:, head_width:] for index in members], axis=0)
        minus = jnp.full(keys.shape, -1.0, jnp.bfloat16)
        scores = dot(jnp.concatenate([keys, minus], axis=1), query_wide, 1, 1)
        probs = jnp.exp2(scores * exponent)
        dprobs = dot(jnp.concatenate([values, minus], axis=1), grad_wide, 1, 1)
        dscores = bf16(probs * dprobs)
        dvalues = dot(bf16(probs), grad, 1, 0)
        dkeys = dot(dscores, query, 1, 0) * score_scale
        for place, index in enumerate(members):
            out = dpairs[index]
            taken = slice(place * key_rows, (place + 1) * key_rows)
            dkey, dvalue = dkeys[taken], dvalues[taken]
            if carried:
                dkey = dkey + before[index][:, :head_width]
                dvalue = dvalue + before[index][:, head_width:]
            out[:, :head_width] = dkey.astype(out.dtype)
            out[:, head_width:] = dvalue.astype(out.dtype)
        dquery = dot(keys, dscores, 0, 0).T * score_scale
        for member in range(group_heads):
            part = dquery[member * all_rows : (member + 1) * all_rows]
            columns = slice((head + member) * head_width, (head + member + 1) * head_width)
            dq_own[:, columns] = part[:half]
            dq_other[:, columns] = bf16(part[half:])


def attend(rows, order, pairs, before, kinds, heads, groups, score_scale):
    block_rows, packed = rows[0].shape
    width = (packed - LANES) // 2
    half = len(order) // 2 * block_rows
    key_rows, head_width = pairs[0].shape[0], pairs[0].shape[1] // 2
    outs = [
        jax.ShapeDtypeStruct((half, width), jnp.float32),
        jax.ShapeDtypeStruct((half, width), jnp.bfloat16),
    ] + [jax.ShapeDtypeStruct(pairs[0].shape, kind) for kind in kinds]
    operands = list(rows) + list(pairs) + list(before)
    products = len(pairs) * key_rows * (heads // groups) * 2 * half
    return pl.pallas_call(
        functools.partial(
            attend_kernel, heads, groups, score_scale, len(rows), order, len(pairs), bool(before)
        ),
        out_shape=tuple(outs),
        in_specs=vmem(len(operands)),
        out_specs=tuple(vmem(len(outs))),
        compiler_params=pltpu.CompilerParams(vmem_limit_bytes=VMEM_BYTES),
        cost_estimate=pl.CostEstimate(
            flops=10 * products * head_width, bytes_accessed=0, transcendentals=products
        ),
    )(*operands)


def finish_kernel(groups, terms, *refs):
    query_terms, pair_terms = refs[:terms], refs[terms : 2 * terms]
    grad_queries, grad_keys, grad_values, queries_block, keys_block, values_block, done = refs[2 * terms :]
    group = lax.axis_index("kv")
    group_width = queries_block.shape[1] // groups
    head_width = keys_block.shape[1]

    def total(parts, columns):
        return functools.reduce(lambda left, right: left + right, [f32(part[:, columns]) for part in parts])

    copies = []
    for block, target, columns in (
        (keys_block, grad_keys, slice(0, head_width)),
        (values_block, grad_values, slice(head_width, 2 * head_width)),
    ):
        block[...] = bf16(total(pair_terms, columns))
        copies.append(pltpu.make_async_copy(block, target, done.at[len(copies)]))
        copies[-1].start()
    for step in range(groups):
        columns = slice(step * group_width, (step + 1) * group_width)
        queries_block[:, columns] = bf16(total(query_terms, columns))
        target = lax.rem(group + step, groups) * group_width
        target = grad_queries.at[:, pl.ds(pl.multiple_of(target, group_width), group_width)]
        source = queries_block.at[:, pl.ds(step * group_width, group_width)]
        copies.append(pltpu.make_async_copy(source, target, done.at[len(copies)]))
        copies[-1].start()
    for copy in copies:
        copy.wait()


def finish(query_terms, pair_terms, groups):
    own_rows, width = query_terms[0].shape
    key_rows, head_width = pair_terms[0].shape[0], pair_terms[0].shape[1] // 2
    shapes = ((own_rows, width), (key_rows, head_width), (key_rows, head_width))
    operands = list(query_terms) + list(pair_terms)
    return pl.pallas_call(
        functools.partial(finish_kernel, groups, len(query_terms)),
        out_shape=tuple(pltpu.HBM(shape, jnp.bfloat16) for shape in shapes),
        in_specs=vmem(len(operands)),
        out_specs=tuple([pl.BlockSpec(memory_space=pltpu.HBM)] * 3),
        scratch_shapes=[pltpu.VMEM(shape, jnp.bfloat16) for shape in shapes]
        + [pltpu.SemaphoreType.DMA((groups + 2,))],
        compiler_params=pltpu.CompilerParams(vmem_limit_bytes=VMEM_BYTES),
    )(*operands)


def turn_seq(array, seq_count, target):
    return lax.ppermute(array, "seq", [(place, target(place)) for place in range(seq_count)])


def planes(queries, out_grad, saved_out, saved_lse, video_keys, video_values):
    groups = lax.axis_size("kv")
    seq_count = lax.axis_size("seq")
    own_rows, width = queries.shape
    heads = saved_lse.shape[1]
    head_width = video_keys.shape[1]
    score_scale = 1.0 / math.sqrt(head_width)

    def steps(array, even, odd):
        return turn_seq(array, seq_count, lambda place: place ^ (4 * (odd if place % 2 else even)))

    def other_core(array):
        return turn_seq(array, seq_count, lambda place: place ^ 1)

    def middle(array):
        return turn_seq(array, seq_count, lambda place: place ^ 2)

    def across(array):
        return lax.ppermute(array, "kv", [(0, 1), (1, 0)])

    def diagonal(array):
        steps = [
            (kv * seq_count + place, (1 - kv) * seq_count + (place ^ 2))
            for kv in range(2)
            for place in range(seq_count)
        ]
        return lax.ppermute(array, ("kv", "seq"), steps)

    packed, pair = pack(
        queries, out_grad, saved_out, saved_lse.T, video_keys, video_values, groups, score_scale
    )
    pair_across, pair_middle = across(pair), middle(pair)
    keys_far = middle(pair_across[:, :head_width])
    values_far = across(pair_middle[:, head_width:])
    pairs = [pair, pair_middle, pair_across, jnp.concatenate([keys_far, values_far], axis=1)]
    beside = other_core(packed)
    from_far = steps(packed, 3, 3)
    from_near = steps(jnp.concatenate([packed, beside], axis=0), 1, 2)
    rows = [packed, beside, from_near, other_core(from_near), from_far, other_core(from_far)]
    order = ((0, 0), (2, 0), (3, 1), (4, 0), (1, 0), (3, 0), (2, 1), (5, 0))
    kinds = [jnp.float32] + [jnp.bfloat16] * 3
    dq_own, dq_other, *dpairs = attend(rows, order, pairs, [], kinds, heads, groups, score_scale)
    arrived = other_core(dq_other)
    dq = (dq_own + f32(arrived)).reshape(-1, own_rows, width)
    dq, dpairs[3] = lax.optimization_barrier((dq, dpairs[3]))
    pair_terms = [dpairs[0], middle(dpairs[1]), across(dpairs[2]), diagonal(dpairs[3])]
    returned = [bf16(dq[place]) for place in range(4)]
    returned[1], pair_terms[2] = lax.optimization_barrier((returned[1], pair_terms[2]))
    query_terms = [
        dq[0], steps(returned[1], 1, 2), steps(returned[2], 2, 1), steps(returned[3], 3, 3)
    ]
    return finish(query_terms, pair_terms, groups)


def head_columns(block, first, width):
    return lax.dynamic_slice_in_dim(block, first, width, 1)


def seq_major(block, kv_count, seq_count):
    total_rows = block.shape[0]
    width = block.shape[1]
    shaped = block.reshape(kv_count, seq_count, total_rows // (kv_count * seq_count), width)
    return shaped.transpose(1, 0, 2, 3).reshape(total_rows, width)


def make_accumulate(
    lse_group,
    delta_group,
    group_index,
    group_width,
    group_heads,
    head_width,
    score_scale,
    video_keys,
    video_values,
):

    def accumulate(totals, pieces, offset):
        key_total, value_total, query_rows = totals
        query_block, grad_block = pieces
        query_block = head_columns(query_block, group_index * group_width, group_width)
        grad_block = head_columns(grad_block, group_index * group_width, group_width)
        columns = []
        for member in range(group_heads):
            query_head = query_block[:, member * head_width : (member + 1) * head_width]
            grad_head = grad_block[:, member * head_width : (member + 1) * head_width]
            scores = (
                jnp.einsum("nd,kd->nk", query_head, video_keys, preferred_element_type=jnp.float32)
                * score_scale
            )
            probs = jnp.exp(scores - lse_group[:, member : member + 1])
            probs_half = probs.astype(jnp.bfloat16)
            value_total = value_total + jnp.einsum(
                "nk,nd->kd", probs_half, grad_head, preferred_element_type=jnp.float32
            )
            dprobs = jnp.einsum(
                "nd,kd->nk", grad_head, video_values, preferred_element_type=jnp.float32
            )
            dscores = (probs * (dprobs - delta_group[:, member : member + 1])).astype(jnp.bfloat16)
            key_total = key_total + jnp.einsum(
                "nk,nd->kd", dscores, query_head, preferred_element_type=jnp.float32
            )
            columns.append(
                jnp.einsum("nk,kd->nd", dscores, video_keys, preferred_element_type=jnp.float32)
            )
        query_rows = jnp.concatenate(columns, axis=1)
        return (key_total, value_total, query_rows)

    return accumulate


def shards(queries, out_grad, saved_out, saved_lse, video_keys, video_values):
    kv_count = lax.axis_size("kv")
    seq_count = lax.axis_size("seq")
    group_index = lax.axis_index("kv")
    head_width = video_keys.shape[1]
    group_heads = saved_lse.shape[1] // kv_count
    group_width = group_heads * head_width
    own_rows = queries.shape[0]
    total_rows = own_rows * kv_count * seq_count
    score_scale = 1.0 / math.sqrt(head_width)
    products = out_grad.astype(jnp.float32) * saved_out.astype(jnp.float32)
    own_delta = products.reshape(own_rows, -1, head_width).sum(axis=2)
    lse_all, delta_all = (
        lax.all_gather(saved_lse, ("kv", "seq"), axis=0, tiled=True),
        lax.all_gather(own_delta, ("kv", "seq"), axis=0, tiled=True),
    )
    lse_wide = head_columns(lse_all, group_index * group_heads, group_heads)
    delta_wide = head_columns(delta_all, group_index * group_heads, group_heads)
    key_rows = video_keys.shape[0]
    initial = (
        jnp.zeros((key_rows, head_width), jnp.float32),
        jnp.zeros((key_rows, head_width), jnp.float32),
        jnp.zeros((total_rows, group_width), jnp.float32),
    )
    wide_step = make_accumulate(
        lse_wide,
        delta_wide,
        group_index,
        group_width,
        group_heads,
        head_width,
        score_scale,
        video_keys,
        video_values,
    )
    gathered = (
        lax.all_gather(queries, ("kv", "seq"), axis=0, tiled=True),
        lax.all_gather(out_grad, ("kv", "seq"), axis=0, tiled=True),
    )
    key_total, value_total, query_rows = wide_step(initial, gathered, 0)
    query_rows = seq_major(query_rows, kv_count, seq_count)
    summed = lax.psum_scatter(
        query_rows.reshape(seq_count, total_rows // seq_count, group_width),
        "seq",
        scatter_dimension=0,
        tiled=True,
    )
    rounded = (summed * score_scale).astype(jnp.bfloat16).reshape(kv_count, own_rows, group_width)
    returned = lax.all_to_all(rounded, "kv", split_axis=0, concat_axis=2, tiled=True)
    grad_queries = returned.reshape(own_rows, kv_count * group_width)
    return (
        grad_queries,
        (key_total * score_scale).astype(jnp.bfloat16),
        value_total.astype(jnp.bfloat16),
    )


def fits_planes(kv_count, seq_count, args):
    queries, _, _, saved_lse, video_keys, _ = args
    return (
        kv_count == 2
        and seq_count == 16
        and queries.shape[0] % 16 == 0
        and queries.shape[0] < LANES
        and video_keys.shape[0] % 16 == 0
        and video_keys.shape[1] == LANES
        and 2 * PIECES * saved_lse.shape[1] <= LANES
    )


def program(*args):
    if fits_planes(lax.axis_size("kv"), lax.axis_size("seq"), args):
        return planes(*args)
    return shards(*args)


def solution(mesh):
    return jax.shard_map(
        program,
        mesh=mesh,
        in_specs=(
            P(("kv", "seq"), None),
            P(("kv", "seq"), None),
            P(("kv", "seq"), None),
            P(("kv", "seq"), None),
            P("seq", "kv"),
            P("seq", "kv"),
        ),
        out_specs=(P(("kv", "seq"), None), P("seq", "kv"), P("seq", "kv")),
        check_vma=False,
    )
```

```python
import functools
import math

import jax
import jax.numpy as jnp
from jax import lax
from jax.experimental import pallas as pl
from jax.experimental.pallas import tpu as pltpu
from jax.sharding import PartitionSpec as P

LANES = 128
PIECES = 3
VMEM_BYTES = 32 * 1024 * 1024


def vmem(count):
    return [pl.BlockSpec(memory_space=pltpu.VMEM)] * count


def bf16(value):
    return value.astype(jnp.bfloat16)


def f32(value):
    return value.astype(jnp.float32)


def pack_kernel(
    heads, groups, score_scale,
    queries, out_grad, saved_out, saved_lse, keys, values,
    rows_out, pairs_out, saved_block, lse_block, done,
):
    own_rows, width = queries.shape
    group_width = width // groups
    group_heads = heads // groups
    head_width = width // heads
    group = lax.axis_index("kv")
    moves = [(saved_lse, lse_block)]
    for step in range(groups):
        source = lax.rem(group + step, groups)
        columns = pl.ds(pl.multiple_of(source * group_width, group_width), group_width)
        target = step * group_width
        moves.append((out_grad.at[:, columns], rows_out.at[:, pl.ds(width + target, group_width)]))
        moves.append((saved_out.at[:, columns], saved_block.at[:, pl.ds(target, group_width)]))
    needed = len(moves)
    for step in range(groups):
        source = lax.rem(group + step, groups)
        columns = pl.ds(pl.multiple_of(source * group_width, group_width), group_width)
        moves.append((queries.at[:, columns], rows_out.at[:, pl.ds(step * group_width, group_width)]))
    moves.append((keys, pairs_out.at[:, pl.ds(0, head_width)]))
    moves.append((values, pairs_out.at[:, pl.ds(head_width, head_width)]))
    copies = [
        pltpu.make_async_copy(source, target, done.at[index])
        for index, (source, target) in enumerate(moves)
    ]
    for copy in copies:
        copy.start()
    lane = lax.broadcasted_iota(jnp.int32, (own_rows, LANES), 1)
    piece = lax.rem(lane, PIECES)
    stats = jnp.zeros((own_rows, LANES), jnp.float32)
    copies[0].wait()
    shifts = jnp.concatenate(
        [lse_block[...], jnp.zeros((heads, LANES - own_rows), jnp.float32)], axis=1
    ).T[:own_rows] * (1.0 / score_scale)
    for copy in copies[1:needed]:
        copy.wait()
    for head in range(heads):
        columns = slice(head * head_width, (head + 1) * head_width)
        grad_columns = slice(width + head * head_width, width + (head + 1) * head_width)
        products = f32(rows_out[:, grad_columns]) * f32(saved_block[:, columns])
        delta = jnp.sum(products, axis=1, keepdims=True)
        place = (heads + head) * PIECES
        stats = jnp.where((lane >= place) & (lane < place + PIECES), delta, stats)
        place = lax.rem(head - group * group_heads + heads, heads) * PIECES
        stats = jnp.where((lane >= place) & (lane < place + PIECES), shifts[:, head : head + 1], stats)
    first = f32(bf16(stats))
    second = f32(bf16(stats - first))
    third = stats - first - second
    rows_out[:, 2 * width :] = bf16(jnp.where(piece == 0, first, jnp.where(piece == 1, second, third)))
    for copy in copies[needed:]:
        copy.wait()


def pack(queries, out_grad, saved_out, saved_lse, keys, values, groups, score_scale):
    own_rows, width = queries.shape
    heads = saved_lse.shape[0]
    return pl.pallas_call(
        functools.partial(pack_kernel, heads, groups, score_scale),
        out_shape=(
            jax.ShapeDtypeStruct((own_rows, 2 * width + LANES), jnp.bfloat16),
            jax.ShapeDtypeStruct((keys.shape[0], 2 * keys.shape[1]), jnp.bfloat16),
        ),
        in_specs=[pl.BlockSpec(memory_space=pltpu.HBM)] * 6,
        out_specs=tuple(vmem(2)),
        scratch_shapes=[
            pltpu.VMEM((own_rows, width), jnp.bfloat16),
            pltpu.VMEM(saved_lse.shape, jnp.float32),
            pltpu.SemaphoreType.DMA((3 * groups + 3,)),
        ],
        compiler_params=pltpu.CompilerParams(vmem_limit_bytes=VMEM_BYTES),
    )(*[
        pltpu.with_memory_space_constraint(array, pltpu.HBM)
        for array in (queries, out_grad, saved_out, saved_lse, keys, values)
    ])


def dot(left, right, left_dim, right_dim):
    return lax.dot_general(
        left, right, (((left_dim,), (right_dim,)), ((), ())), preferred_element_type=jnp.float32
    )


def attend_kernel(heads, groups, score_scale, arrays, order, pair_count, carried, *refs):
    refs = list(refs)
    held = [refs.pop(0) for _ in range(arrays)]
    pairs = [refs.pop(0) for _ in range(pair_count)]
    before = [refs.pop(0) for _ in range(pair_count)] if carried else None
    dq_own, dq_other, *dpairs = refs
    block_rows = held[0].shape[0]
    width = (held[0].shape[1] - LANES) // 2
    head_width = width // heads
    group_heads = heads // groups
    all_rows = len(order) * block_rows
    half = all_rows // 2
    rows = [held[array].at[pl.ds(place * block_rows, block_rows)] for array, place in order]
    key_rows = pairs[0].shape[0]
    per_group = pair_count // groups
    exponent = score_scale * math.log2(math.e)
    lane = lax.broadcasted_iota(jnp.int32, (all_rows, LANES), 1)
    stats = jnp.concatenate([block[:, 2 * width :] for block in rows], axis=0)
    none = jnp.zeros_like(stats)

    def stacked(start):
        return jnp.concatenate(
            [
                block[:, start + member * head_width : start + (member + 1) * head_width]
                for member in range(group_heads)
                for block in rows
            ],
            axis=0,
        )

    def picked(first):
        firsts = [first + member * PIECES for member in range(group_heads)]
        return jnp.concatenate(
            [jnp.where((lane >= place) & (lane < place + PIECES), stats, none) for place in firsts], axis=0
        )

    for group in range(groups):
        head = group * group_heads
        query = stacked(head * head_width)
        grad = stacked(width + head * head_width)
        query_wide = jnp.concatenate([query, picked(head * PIECES)], axis=1)
        grad_wide = jnp.concatenate([grad, picked((heads + head) * PIECES)], axis=1)
        members = range(group * per_group, (group + 1) * per_group)
        keys = jnp.concatenate([pairs[index][:, :head_width] for index in members], axis=0)
        values = jnp.concatenate([pairs[index][:, head_width:] for index in members], axis=0)
        minus = jnp.full(keys.shape, -1.0, jnp.bfloat16)
        scores = dot(jnp.concatenate([keys, minus], axis=1), query_wide, 1, 1)
        probs = jnp.exp2(scores * exponent)
        dprobs = dot(jnp.concatenate([values, minus], axis=1), grad_wide, 1, 1)
        dscores = bf16(probs * dprobs)
        dvalues = dot(bf16(probs), grad, 1, 0)
        dkeys = dot(dscores, query, 1, 0) * score_scale
        for place, index in enumerate(members):
            out = dpairs[index]
            taken = slice(place * key_rows, (place + 1) * key_rows)
            dkey, dvalue = dkeys[taken], dvalues[taken]
            if carried:
                dkey = dkey + before[index][:, :head_width]
                dvalue = dvalue + before[index][:, head_width:]
            out[:, :head_width] = dkey.astype(out.dtype)
            out[:, head_width:] = dvalue.astype(out.dtype)
        dquery = dot(keys, dscores, 0, 0).T * score_scale
        for member in range(group_heads):
            part = dquery[member * all_rows : (member + 1) * all_rows]
            columns = slice((head + member) * head_width, (head + member + 1) * head_width)
            dq_own[:, columns] = part[:half]
            dq_other[:, columns] = bf16(part[half:])


def attend(rows, order, pairs, before, kinds, heads, groups, score_scale):
    block_rows, packed = rows[0].shape
    width = (packed - LANES) // 2
    half = len(order) // 2 * block_rows
    key_rows, head_width = pairs[0].shape[0], pairs[0].shape[1] // 2
    outs = [
        jax.ShapeDtypeStruct((half, width), jnp.float32),
        jax.ShapeDtypeStruct((half, width), jnp.bfloat16),
    ] + [jax.ShapeDtypeStruct(pairs[0].shape, kind) for kind in kinds]
    operands = list(rows) + list(pairs) + list(before)
    products = len(pairs) * key_rows * (heads // groups) * 2 * half
    return pl.pallas_call(
        functools.partial(
            attend_kernel, heads, groups, score_scale, len(rows), order, len(pairs), bool(before)
        ),
        out_shape=tuple(outs),
        in_specs=vmem(len(operands)),
        out_specs=tuple(vmem(len(outs))),
        compiler_params=pltpu.CompilerParams(vmem_limit_bytes=VMEM_BYTES),
        cost_estimate=pl.CostEstimate(
            flops=10 * products * head_width, bytes_accessed=0, transcendentals=products
        ),
    )(*operands)


def finish_kernel(groups, terms, *refs):
    query_terms, pair_terms = refs[:terms], refs[terms : 2 * terms]
    grad_queries, grad_keys, grad_values, queries_block, keys_block, values_block, done = refs[2 * terms :]
    group = lax.axis_index("kv")
    group_width = queries_block.shape[1] // groups
    head_width = keys_block.shape[1]

    def total(parts, columns):
        return functools.reduce(lambda left, right: left + right, [f32(part[:, columns]) for part in parts])

    copies = []
    for block, target, columns in (
        (keys_block, grad_keys, slice(0, head_width)),
        (values_block, grad_values, slice(head_width, 2 * head_width)),
    ):
        block[...] = bf16(total(pair_terms, columns))
        copies.append(pltpu.make_async_copy(block, target, done.at[len(copies)]))
        copies[-1].start()
    for step in range(groups):
        columns = slice(step * group_width, (step + 1) * group_width)
        queries_block[:, columns] = bf16(total(query_terms, columns))
        target = lax.rem(group + step, groups) * group_width
        target = grad_queries.at[:, pl.ds(pl.multiple_of(target, group_width), group_width)]
        source = queries_block.at[:, pl.ds(step * group_width, group_width)]
        copies.append(pltpu.make_async_copy(source, target, done.at[len(copies)]))
        copies[-1].start()
    for copy in copies:
        copy.wait()


def finish(query_terms, pair_terms, groups):
    own_rows, width = query_terms[0].shape
    key_rows, head_width = pair_terms[0].shape[0], pair_terms[0].shape[1] // 2
    shapes = ((own_rows, width), (key_rows, head_width), (key_rows, head_width))
    operands = list(query_terms) + list(pair_terms)
    return pl.pallas_call(
        functools.partial(finish_kernel, groups, len(query_terms)),
        out_shape=tuple(pltpu.HBM(shape, jnp.bfloat16) for shape in shapes),
        in_specs=vmem(len(operands)),
        out_specs=tuple([pl.BlockSpec(memory_space=pltpu.HBM)] * 3),
        scratch_shapes=[pltpu.VMEM(shape, jnp.bfloat16) for shape in shapes]
        + [pltpu.SemaphoreType.DMA((groups + 2,))],
        compiler_params=pltpu.CompilerParams(vmem_limit_bytes=VMEM_BYTES),
    )(*operands)


def turn_seq(array, seq_count, target):
    return lax.ppermute(array, "seq", [(place, target(place)) for place in range(seq_count)])


def planes(queries, out_grad, saved_out, saved_lse, video_keys, video_values):
    groups = lax.axis_size("kv")
    seq_count = lax.axis_size("seq")
    own_rows, width = queries.shape
    heads = saved_lse.shape[1]
    head_width = video_keys.shape[1]
    score_scale = 1.0 / math.sqrt(head_width)

    def steps(array, even, odd):
        return turn_seq(array, seq_count, lambda place: place ^ (4 * (odd if place % 2 else even)))

    def other_core(array):
        return turn_seq(array, seq_count, lambda place: place ^ 1)

    def middle(array):
        return turn_seq(array, seq_count, lambda place: place ^ 2)

    def across(array):
        return lax.ppermute(array, "kv", [(0, 1), (1, 0)])

    def diagonal(array):
        steps = [
            (kv * seq_count + place, (1 - kv) * seq_count + (place ^ 2))
            for kv in range(2)
            for place in range(seq_count)
        ]
        return lax.ppermute(array, ("kv", "seq"), steps)

    packed, pair = pack(
        queries, out_grad, saved_out, saved_lse.T, video_keys, video_values, groups, score_scale
    )
    pair_across, pair_middle = across(pair), middle(pair)
    keys_far = middle(pair_across[:, :head_width])
    values_far = across(pair_middle[:, head_width:])
    pairs = [pair, pair_middle, pair_across, jnp.concatenate([keys_far, values_far], axis=1)]
    beside = other_core(packed)
    from_far = steps(packed, 3, 3)
    from_near = steps(jnp.concatenate([packed, beside], axis=0), 1, 2)
    rows = [packed, beside, from_near, other_core(from_near), from_far, other_core(from_far)]
    order = ((0, 0), (2, 0), (3, 1), (4, 0), (1, 0), (3, 0), (2, 1), (5, 0))
    kinds = [jnp.float32] + [jnp.bfloat16] * 3
    dq_own, dq_other, *dpairs = attend(rows, order, pairs, [], kinds, heads, groups, score_scale)
    arrived = other_core(dq_other)
    dq = (dq_own + f32(arrived)).reshape(-1, own_rows, width)
    dq, dpairs[3] = lax.optimization_barrier((dq, dpairs[3]))
    pair_terms = [dpairs[0], middle(dpairs[1]), across(dpairs[2]), diagonal(dpairs[3])]
    returned = [bf16(dq[place]) for place in range(4)]
    returned[1], pair_terms[2] = lax.optimization_barrier((returned[1], pair_terms[2]))
    query_terms = [
        dq[0], steps(returned[1], 1, 2), steps(returned[2], 2, 1), steps(returned[3], 3, 3)
    ]
    return finish(query_terms, pair_terms, groups)


def head_columns(block, first, width):
    return lax.dynamic_slice_in_dim(block, first, width, 1)


def seq_major(block, kv_count, seq_count):
    total_rows = block.shape[0]
    width = block.shape[1]
    shaped = block.reshape(kv_count, seq_count, total_rows // (kv_count * seq_count), width)
    return shaped.transpose(1, 0, 2, 3).reshape(total_rows, width)


def make_accumulate(
    lse_group,
    delta_group,
    group_index,
    group_width,
    group_heads,
    head_width,
    score_scale,
    video_keys,
    video_values,
):

    def accumulate(totals, pieces, offset):
        key_total, value_total, query_rows = totals
        query_block, grad_block = pieces
        query_block = head_columns(query_block, group_index * group_width, group_width)
        grad_block = head_columns(grad_block, group_index * group_width, group_width)
        columns = []
        for member in range(group_heads):
            query_head = query_block[:, member * head_width : (member + 1) * head_width]
            grad_head = grad_block[:, member * head_width : (member + 1) * head_width]
            scores = (
                jnp.einsum("nd,kd->nk", query_head, video_keys, preferred_element_type=jnp.float32)
                * score_scale
            )
            probs = jnp.exp(scores - lse_group[:, member : member + 1])
            probs_half = probs.astype(jnp.bfloat16)
            value_total = value_total + jnp.einsum(
                "nk,nd->kd", probs_half, grad_head, preferred_element_type=jnp.float32
            )
            dprobs = jnp.einsum(
                "nd,kd->nk", grad_head, video_values, preferred_element_type=jnp.float32
            )
            dscores = (probs * (dprobs - delta_group[:, member : member + 1])).astype(jnp.bfloat16)
            key_total = key_total + jnp.einsum(
                "nk,nd->kd", dscores, query_head, preferred_element_type=jnp.float32
            )
            columns.append(
                jnp.einsum("nk,kd->nd", dscores, video_keys, preferred_element_type=jnp.float32)
            )
        query_rows = jnp.concatenate(columns, axis=1)
        return (key_total, value_total, query_rows)

    return accumulate


def shards(queries, out_grad, saved_out, saved_lse, video_keys, video_values):
    kv_count = lax.axis_size("kv")
    seq_count = lax.axis_size("seq")
    group_index = lax.axis_index("kv")
    head_width = video_keys.shape[1]
    group_heads = saved_lse.shape[1] // kv_count
    group_width = group_heads * head_width
    own_rows = queries.shape[0]
    total_rows = own_rows * kv_count * seq_count
    score_scale = 1.0 / math.sqrt(head_width)
    products = out_grad.astype(jnp.float32) * saved_out.astype(jnp.float32)
    own_delta = products.reshape(own_rows, -1, head_width).sum(axis=2)
    lse_all, delta_all = (
        lax.all_gather(saved_lse, ("kv", "seq"), axis=0, tiled=True),
        lax.all_gather(own_delta, ("kv", "seq"), axis=0, tiled=True),
    )
    lse_wide = head_columns(lse_all, group_index * group_heads, group_heads)
    delta_wide = head_columns(delta_all, group_index * group_heads, group_heads)
    key_rows = video_keys.shape[0]
    initial = (
        jnp.zeros((key_rows, head_width), jnp.float32),
        jnp.zeros((key_rows, head_width), jnp.float32),
        jnp.zeros((total_rows, group_width), jnp.float32),
    )
    wide_step = make_accumulate(
        lse_wide,
        delta_wide,
        group_index,
        group_width,
        group_heads,
        head_width,
        score_scale,
        video_keys,
        video_values,
    )
    gathered = (
        lax.all_gather(queries, ("kv", "seq"), axis=0, tiled=True),
        lax.all_gather(out_grad, ("kv", "seq"), axis=0, tiled=True),
    )
    key_total, value_total, query_rows = wide_step(initial, gathered, 0)
    query_rows = seq_major(query_rows, kv_count, seq_count)
    summed = lax.psum_scatter(
        query_rows.reshape(seq_count, total_rows // seq_count, group_width),
        "seq",
        scatter_dimension=0,
        tiled=True,
    )
    rounded = (summed * score_scale).astype(jnp.bfloat16).reshape(kv_count, own_rows, group_width)
    returned = lax.all_to_all(rounded, "kv", split_axis=0, concat_axis=2, tiled=True)
    grad_queries = returned.reshape(own_rows, kv_count * group_width)
    return (
        grad_queries,
        (key_total * score_scale).astype(jnp.bfloat16),
        value_total.astype(jnp.bfloat16),
    )


def fits_planes(kv_count, seq_count, args):
    queries, _, _, saved_lse, video_keys, _ = args
    return (
        kv_count == 2
        and seq_count == 16
        and queries.shape[0] % 16 == 0
        and queries.shape[0] < LANES
        and video_keys.shape[0] % 16 == 0
        and video_keys.shape[1] == LANES
        and 2 * PIECES * saved_lse.shape[1] <= LANES
    )


def program(*args):
    if fits_planes(lax.axis_size("kv"), lax.axis_size("seq"), args):
        return planes(*args)
    return shards(*args)


def solution(mesh):
    return jax.shard_map(
        program,
        mesh=mesh,
        in_specs=(
            P(("kv", "seq"), None),
            P(("kv", "seq"), None),
            P(("kv", "seq"), None),
            P(("kv", "seq"), None),
            P("seq", "kv"),
            P("seq", "kv"),
        ),
        out_specs=(P(("kv", "seq"), None), P("seq", "kv"), P("seq", "kv")),
        check_vma=False,
    )
```

```python
import functools
import math

import jax
import jax.numpy as jnp
from jax import lax
from jax.experimental import pallas as pl
from jax.experimental.pallas import tpu as pltpu
from jax.sharding import PartitionSpec as P

LANES = 128
PIECES = 3
VMEM_BYTES = 32 * 1024 * 1024


def vmem(count):
    return [pl.BlockSpec(memory_space=pltpu.VMEM)] * count


def bf16(value):
    return value.astype(jnp.bfloat16)


def f32(value):
    return value.astype(jnp.float32)


def pack_kernel(
    heads, groups, score_scale,
    queries, out_grad, saved_out, saved_lse, keys, values,
    rows_out, pairs_out, saved_block, lse_block, done,
):
    own_rows, width = queries.shape
    group_width = width // groups
    group_heads = heads // groups
    head_width = width // heads
    group = lax.axis_index("kv")
    moves = [(saved_lse, lse_block)]
    for step in range(groups):
        source = lax.rem(group + step, groups)
        columns = pl.ds(pl.multiple_of(source * group_width, group_width), group_width)
        target = step * group_width
        moves.append((out_grad.at[:, columns], rows_out.at[:, pl.ds(width + target, group_width)]))
        moves.append((saved_out.at[:, columns], saved_block.at[:, pl.ds(target, group_width)]))
    needed = len(moves)
    for step in range(groups):
        source = lax.rem(group + step, groups)
        columns = pl.ds(pl.multiple_of(source * group_width, group_width), group_width)
        moves.append((queries.at[:, columns], rows_out.at[:, pl.ds(step * group_width, group_width)]))
    moves.append((keys, pairs_out.at[:, pl.ds(0, head_width)]))
    moves.append((values, pairs_out.at[:, pl.ds(head_width, head_width)]))
    copies = [
        pltpu.make_async_copy(source, target, done.at[index])
        for index, (source, target) in enumerate(moves)
    ]
    for copy in copies:
        copy.start()
    lane = lax.broadcasted_iota(jnp.int32, (own_rows, LANES), 1)
    piece = lax.rem(lane, PIECES)
    stats = jnp.zeros((own_rows, LANES), jnp.float32)
    for copy in copies[:needed]:
        copy.wait()
    shifts = jnp.concatenate(
        [lse_block[...], jnp.zeros((heads, LANES - own_rows), jnp.float32)], axis=1
    ).T[:own_rows] * (1.0 / score_scale)
    for head in range(heads):
        columns = slice(head * head_width, (head + 1) * head_width)
        grad_columns = slice(width + head * head_width, width + (head + 1) * head_width)
        products = f32(rows_out[:, grad_columns]) * f32(saved_block[:, columns])
        delta = jnp.sum(products, axis=1, keepdims=True)
        place = (heads + head) * PIECES
        stats = jnp.where((lane >= place) & (lane < place + PIECES), delta, stats)
        place = lax.rem(head - group * group_heads + heads, heads) * PIECES
        stats = jnp.where((lane >= place) & (lane < place + PIECES), shifts[:, head : head + 1], stats)
    first = f32(bf16(stats))
    second = f32(bf16(stats - first))
    third = stats - first - second
    rows_out[:, 2 * width :] = bf16(jnp.where(piece == 0, first, jnp.where(piece == 1, second, third)))
    for copy in copies[needed:]:
        copy.wait()


def pack(queries, out_grad, saved_out, saved_lse, keys, values, groups, score_scale):
    own_rows, width = queries.shape
    heads = saved_lse.shape[0]
    return pl.pallas_call(
        functools.partial(pack_kernel, heads, groups, score_scale),
        out_shape=(
            jax.ShapeDtypeStruct((own_rows, 2 * width + LANES), jnp.bfloat16),
            jax.ShapeDtypeStruct((keys.shape[0], 2 * keys.shape[1]), jnp.bfloat16),
        ),
        in_specs=[pl.BlockSpec(memory_space=pltpu.HBM)] * 6,
        out_specs=tuple(vmem(2)),
        scratch_shapes=[
            pltpu.VMEM((own_rows, width), jnp.bfloat16),
            pltpu.VMEM(saved_lse.shape, jnp.float32),
            pltpu.SemaphoreType.DMA((3 * groups + 3,)),
        ],
        compiler_params=pltpu.CompilerParams(vmem_limit_bytes=VMEM_BYTES),
    )(*[
        pltpu.with_memory_space_constraint(array, pltpu.HBM)
        for array in (queries, out_grad, saved_out, saved_lse, keys, values)
    ])


def dot(left, right, left_dim, right_dim):
    return lax.dot_general(
        left, right, (((left_dim,), (right_dim,)), ((), ())), preferred_element_type=jnp.float32
    )


def attend_kernel(heads, groups, score_scale, arrays, order, pair_count, carried, *refs):
    refs = list(refs)
    held = [refs.pop(0) for _ in range(arrays)]
    pairs = [refs.pop(0) for _ in range(pair_count)]
    before = [refs.pop(0) for _ in range(pair_count)] if carried else None
    dq_own, dq_other, *dpairs = refs
    block_rows = held[0].shape[0]
    width = (held[0].shape[1] - LANES) // 2
    head_width = width // heads
    group_heads = heads // groups
    all_rows = len(order) * block_rows
    half = all_rows // 2
    rows = [held[array].at[pl.ds(place * block_rows, block_rows)] for array, place in order]
    key_rows = pairs[0].shape[0]
    per_group = pair_count // groups
    exponent = score_scale * math.log2(math.e)
    lane = lax.broadcasted_iota(jnp.int32, (all_rows, LANES), 1)
    stats = jnp.concatenate([block[:, 2 * width :] for block in rows], axis=0)
    none = jnp.zeros_like(stats)

    def stacked(start):
        return jnp.concatenate(
            [
                block[:, start + member * head_width : start + (member + 1) * head_width]
                for member in range(group_heads)
                for block in rows
            ],
            axis=0,
        )

    def picked(first):
        firsts = [first + member * PIECES for member in range(group_heads)]
        return jnp.concatenate(
            [jnp.where((lane >= place) & (lane < place + PIECES), stats, none) for place in firsts], axis=0
        )

    for group in range(groups):
        head = group * group_heads
        query = stacked(head * head_width)
        grad = stacked(width + head * head_width)
        query_wide = jnp.concatenate([query, picked(head * PIECES)], axis=1)
        grad_wide = jnp.concatenate([grad, picked((heads + head) * PIECES)], axis=1)
        members = range(group * per_group, (group + 1) * per_group)
        keys = jnp.concatenate([pairs[index][:, :head_width] for index in members], axis=0)
        values = jnp.concatenate([pairs[index][:, head_width:] for index in members], axis=0)
        minus = jnp.full(keys.shape, -1.0, jnp.bfloat16)
        scores = dot(jnp.concatenate([keys, minus], axis=1), query_wide, 1, 1)
        probs = jnp.exp2(scores * exponent)
        dprobs = dot(jnp.concatenate([values, minus], axis=1), grad_wide, 1, 1)
        dscores = bf16(probs * dprobs)
        dvalues = dot(bf16(probs), grad, 1, 0)
        dkeys = dot(dscores, query, 1, 0) * score_scale
        for place, index in enumerate(members):
            out = dpairs[index]
            taken = slice(place * key_rows, (place + 1) * key_rows)
            dkey, dvalue = dkeys[taken], dvalues[taken]
            if carried:
                dkey = dkey + before[index][:, :head_width]
                dvalue = dvalue + before[index][:, head_width:]
            out[:, :head_width] = dkey.astype(out.dtype)
            out[:, head_width:] = dvalue.astype(out.dtype)
        dquery = dot(keys, dscores, 0, 0).T * score_scale
        for member in range(group_heads):
            part = dquery[member * all_rows : (member + 1) * all_rows]
            columns = slice((head + member) * head_width, (head + member + 1) * head_width)
            dq_own[:, columns] = part[:half]
            dq_other[:, columns] = bf16(part[half:])


def attend(rows, order, pairs, before, kinds, heads, groups, score_scale):
    block_rows, packed = rows[0].shape
    width = (packed - LANES) // 2
    half = len(order) // 2 * block_rows
    key_rows, head_width = pairs[0].shape[0], pairs[0].shape[1] // 2
    outs = [
        jax.ShapeDtypeStruct((half, width), jnp.float32),
        jax.ShapeDtypeStruct((half, width), jnp.bfloat16),
    ] + [jax.ShapeDtypeStruct(pairs[0].shape, kind) for kind in kinds]
    operands = list(rows) + list(pairs) + list(before)
    products = len(pairs) * key_rows * (heads // groups) * 2 * half
    return pl.pallas_call(
        functools.partial(
            attend_kernel, heads, groups, score_scale, len(rows), order, len(pairs), bool(before)
        ),
        out_shape=tuple(outs),
        in_specs=vmem(len(operands)),
        out_specs=tuple(vmem(len(outs))),
        compiler_params=pltpu.CompilerParams(vmem_limit_bytes=VMEM_BYTES),
        cost_estimate=pl.CostEstimate(
            flops=10 * products * head_width, bytes_accessed=0, transcendentals=products
        ),
    )(*operands)


def finish_kernel(groups, terms, *refs):
    query_terms, pair_terms = refs[:terms], refs[terms : 2 * terms]
    grad_queries, grad_keys, grad_values, queries_block, keys_block, values_block, done = refs[2 * terms :]
    group = lax.axis_index("kv")
    group_width = queries_block.shape[1] // groups
    head_width = keys_block.shape[1]

    def total(parts, columns):
        return functools.reduce(lambda left, right: left + right, [f32(part[:, columns]) for part in parts])

    copies = []
    for block, target, columns in (
        (keys_block, grad_keys, slice(0, head_width)),
        (values_block, grad_values, slice(head_width, 2 * head_width)),
    ):
        block[...] = bf16(total(pair_terms, columns))
        copies.append(pltpu.make_async_copy(block, target, done.at[len(copies)]))
        copies[-1].start()
    for step in range(groups):
        columns = slice(step * group_width, (step + 1) * group_width)
        queries_block[:, columns] = bf16(total(query_terms, columns))
        target = lax.rem(group + step, groups) * group_width
        target = grad_queries.at[:, pl.ds(pl.multiple_of(target, group_width), group_width)]
        source = queries_block.at[:, pl.ds(step * group_width, group_width)]
        copies.append(pltpu.make_async_copy(source, target, done.at[len(copies)]))
        copies[-1].start()
    for copy in copies:
        copy.wait()


def finish(query_terms, pair_terms, groups):
    own_rows, width = query_terms[0].shape
    key_rows, head_width = pair_terms[0].shape[0], pair_terms[0].shape[1] // 2
    shapes = ((own_rows, width), (key_rows, head_width), (key_rows, head_width))
    operands = list(query_terms) + list(pair_terms)
    return pl.pallas_call(
        functools.partial(finish_kernel, groups, len(query_terms)),
        out_shape=tuple(pltpu.HBM(shape, jnp.bfloat16) for shape in shapes),
        in_specs=vmem(len(operands)),
        out_specs=tuple([pl.BlockSpec(memory_space=pltpu.HBM)] * 3),
        scratch_shapes=[pltpu.VMEM(shape, jnp.bfloat16) for shape in shapes]
        + [pltpu.SemaphoreType.DMA((groups + 2,))],
        compiler_params=pltpu.CompilerParams(vmem_limit_bytes=VMEM_BYTES),
    )(*operands)


def turn_seq(array, seq_count, target):
    return lax.ppermute(array, "seq", [(place, target(place)) for place in range(seq_count)])


def planes(queries, out_grad, saved_out, saved_lse, video_keys, video_values):
    groups = lax.axis_size("kv")
    seq_count = lax.axis_size("seq")
    own_rows, width = queries.shape
    heads = saved_lse.shape[1]
    head_width = video_keys.shape[1]
    score_scale = 1.0 / math.sqrt(head_width)

    def steps(array, even, odd):
        return turn_seq(array, seq_count, lambda place: place ^ (4 * (odd if place % 2 else even)))

    def other_core(array):
        return turn_seq(array, seq_count, lambda place: place ^ 1)

    def middle(array):
        return turn_seq(array, seq_count, lambda place: place ^ 2)

    def across(array):
        return lax.ppermute(array, "kv", [(0, 1), (1, 0)])

    def diagonal(array):
        steps = [
            (kv * seq_count + place, (1 - kv) * seq_count + (place ^ 2))
            for kv in range(2)
            for place in range(seq_count)
        ]
        return lax.ppermute(array, ("kv", "seq"), steps)

    packed, pair = pack(
        queries, out_grad, saved_out, saved_lse.T, video_keys, video_values, groups, score_scale
    )
    pair_across, pair_middle = across(pair), middle(pair)
    values_far = middle(pair_across[:, head_width:])
    keys_far = across(pair_middle[:, :head_width])
    pairs = [pair, pair_middle, pair_across, jnp.concatenate([keys_far, values_far], axis=1)]
    beside = other_core(packed)
    from_far = steps(packed, 3, 3)
    from_near = steps(jnp.concatenate([packed, beside], axis=0), 1, 2)
    rows = [packed, beside, from_near, other_core(from_near), from_far, other_core(from_far)]
    order = ((0, 0), (2, 0), (3, 1), (4, 0), (1, 0), (3, 0), (2, 1), (5, 0))
    kinds = [jnp.float32] + [jnp.bfloat16] * 3
    dq_own, dq_other, *dpairs = attend(rows, order, pairs, [], kinds, heads, groups, score_scale)
    arrived = other_core(dq_other)
    dq = (dq_own + f32(arrived)).reshape(-1, own_rows, width)
    dq, dpairs[3] = lax.optimization_barrier((dq, dpairs[3]))
    pair_terms = [dpairs[0], middle(dpairs[1]), across(dpairs[2]), diagonal(dpairs[3])]
    returned = [bf16(dq[place]) for place in range(4)]
    returned[1], pair_terms[2] = lax.optimization_barrier((returned[1], pair_terms[2]))
    query_terms = [
        dq[0], steps(returned[1], 1, 2), steps(returned[2], 2, 1), steps(returned[3], 3, 3)
    ]
    return finish(query_terms, pair_terms, groups)


def head_columns(block, first, width):
    return lax.dynamic_slice_in_dim(block, first, width, 1)


def seq_major(block, kv_count, seq_count):
    total_rows = block.shape[0]
    width = block.shape[1]
    shaped = block.reshape(kv_count, seq_count, total_rows // (kv_count * seq_count), width)
    return shaped.transpose(1, 0, 2, 3).reshape(total_rows, width)


def make_accumulate(
    lse_group,
    delta_group,
    group_index,
    group_width,
    group_heads,
    head_width,
    score_scale,
    video_keys,
    video_values,
):

    def accumulate(totals, pieces, offset):
        key_total, value_total, query_rows = totals
        query_block, grad_block = pieces
        query_block = head_columns(query_block, group_index * group_width, group_width)
        grad_block = head_columns(grad_block, group_index * group_width, group_width)
        columns = []
        for member in range(group_heads):
            query_head = query_block[:, member * head_width : (member + 1) * head_width]
            grad_head = grad_block[:, member * head_width : (member + 1) * head_width]
            scores = (
                jnp.einsum("nd,kd->nk", query_head, video_keys, preferred_element_type=jnp.float32)
                * score_scale
            )
            probs = jnp.exp(scores - lse_group[:, member : member + 1])
            probs_half = probs.astype(jnp.bfloat16)
            value_total = value_total + jnp.einsum(
                "nk,nd->kd", probs_half, grad_head, preferred_element_type=jnp.float32
            )
            dprobs = jnp.einsum(
                "nd,kd->nk", grad_head, video_values, preferred_element_type=jnp.float32
            )
            dscores = (probs * (dprobs - delta_group[:, member : member + 1])).astype(jnp.bfloat16)
            key_total = key_total + jnp.einsum(
                "nk,nd->kd", dscores, query_head, preferred_element_type=jnp.float32
            )
            columns.append(
                jnp.einsum("nk,kd->nd", dscores, video_keys, preferred_element_type=jnp.float32)
            )
        query_rows = jnp.concatenate(columns, axis=1)
        return (key_total, value_total, query_rows)

    return accumulate


def shards(queries, out_grad, saved_out, saved_lse, video_keys, video_values):
    kv_count = lax.axis_size("kv")
    seq_count = lax.axis_size("seq")
    group_index = lax.axis_index("kv")
    head_width = video_keys.shape[1]
    group_heads = saved_lse.shape[1] // kv_count
    group_width = group_heads * head_width
    own_rows = queries.shape[0]
    total_rows = own_rows * kv_count * seq_count
    score_scale = 1.0 / math.sqrt(head_width)
    products = out_grad.astype(jnp.float32) * saved_out.astype(jnp.float32)
    own_delta = products.reshape(own_rows, -1, head_width).sum(axis=2)
    lse_all, delta_all = (
        lax.all_gather(saved_lse, ("kv", "seq"), axis=0, tiled=True),
        lax.all_gather(own_delta, ("kv", "seq"), axis=0, tiled=True),
    )
    lse_wide = head_columns(lse_all, group_index * group_heads, group_heads)
    delta_wide = head_columns(delta_all, group_index * group_heads, group_heads)
    key_rows = video_keys.shape[0]
    initial = (
        jnp.zeros((key_rows, head_width), jnp.float32),
        jnp.zeros((key_rows, head_width), jnp.float32),
        jnp.zeros((total_rows, group_width), jnp.float32),
    )
    wide_step = make_accumulate(
        lse_wide,
        delta_wide,
        group_index,
        group_width,
        group_heads,
        head_width,
        score_scale,
        video_keys,
        video_values,
    )
    gathered = (
        lax.all_gather(queries, ("kv", "seq"), axis=0, tiled=True),
        lax.all_gather(out_grad, ("kv", "seq"), axis=0, tiled=True),
    )
    key_total, value_total, query_rows = wide_step(initial, gathered, 0)
    query_rows = seq_major(query_rows, kv_count, seq_count)
    summed = lax.psum_scatter(
        query_rows.reshape(seq_count, total_rows // seq_count, group_width),
        "seq",
        scatter_dimension=0,
        tiled=True,
    )
    rounded = (summed * score_scale).astype(jnp.bfloat16).reshape(kv_count, own_rows, group_width)
    returned = lax.all_to_all(rounded, "kv", split_axis=0, concat_axis=2, tiled=True)
    grad_queries = returned.reshape(own_rows, kv_count * group_width)
    return (
        grad_queries,
        (key_total * score_scale).astype(jnp.bfloat16),
        value_total.astype(jnp.bfloat16),
    )


def fits_planes(kv_count, seq_count, args):
    queries, _, _, saved_lse, video_keys, _ = args
    return (
        kv_count == 2
        and seq_count == 16
        and queries.shape[0] % 16 == 0
        and queries.shape[0] < LANES
        and video_keys.shape[0] % 16 == 0
        and video_keys.shape[1] == LANES
        and 2 * PIECES * saved_lse.shape[1] <= LANES
    )


def program(*args):
    if fits_planes(lax.axis_size("kv"), lax.axis_size("seq"), args):
        return planes(*args)
    return shards(*args)


def solution(mesh):
    return jax.shard_map(
        program,
        mesh=mesh,
        in_specs=(
            P(("kv", "seq"), None),
            P(("kv", "seq"), None),
            P(("kv", "seq"), None),
            P(("kv", "seq"), None),
            P("seq", "kv"),
            P("seq", "kv"),
        ),
        out_specs=(P(("kv", "seq"), None), P("seq", "kv"), P("seq", "kv")),
        check_vma=False,
    )
```
